512 devices in a mesh: row: 8 (over y), col: 8 (over z_lo, x), depth: 8 (over z_hi, core).
Axes of the slice: x: 4, y: 8, z: 8 (z_hi: 4, z_lo: 2; z = z_hi * 2 + z_lo), core: 2. Of those that a mesh axis runs over, the one named last changes fastest.
Arguments:
- amplitudes: float32 [32, 32, 512, 512], P('row', 'col', 'depth'), may hold values from -6 to 6
- ladder_ints: float32 [512, 512, 640], P('depth', ('row', 'col')), may hold values from -0.01171875 to 0.01171875
- cycle_ints: float32 [32, 512, 128], P(None, ('row', 'col')), may hold values from -0.125 to 0.125
- occ_irrep: int32 [32], replicated, may hold values from 0 to 7
- vir_irrep: int32 [512], replicated, may hold values from 0 to 7
- pair_irrep: int32 [128], replicated, may hold values from 0 to 7
Outputs:
- ladder_resid: float32 [1024, 640], P(('row', 'col', 'depth'))
- cycle_resid: float32 [32, 512, 128], P(None, 'depth', ('row', 'col'))
The draws below stay inside these ranges and needn't reach their ends.
All inputs are finite; a program needn't handle non-finite values.
Results may differ from the reference program's by a relative error of at most 0.00007.
Values sent between devices are 32-bit elements; how exact they have to be, the bound alone decides.
No kernel may reach another device: no remote copies, remote signals or barrier semaphores. Data moves between devices by JAX's collectives and lax.ppermute only.
A program may use at most 128 MiB of HBM per device.

```python
import jax
import jax.numpy as jnp
from jax import lax

NOCC = 32
NVIR = 512
SLAB = 640
CYCLE_SLAB = 128


def place_ends(drawn, key, least, top_value):
    place = [jax.random.randint(jax.random.fold_in(key, axis), (), 0, length) for axis, length in enumerate(drawn.shape)]
    longest = drawn.shape.index(max(drawn.shape))
    next_to = place[:longest] + [(place[longest] + 1) % drawn.shape[longest]] + place[longest + 1:]
    return drawn.at[tuple(place)].set(least).at[tuple(next_to)].set(top_value)


def level_of(rng, shape, cuts, smallest, largest):
    def one(axis_at, blocks):
        steps = jax.random.uniform(jax.random.fold_in(jax.random.fold_in(rng, 6), axis_at), (blocks,), jnp.float32, smallest / len(cuts), largest / len(cuts))
        return jnp.repeat(jnp.exp(steps), shape[axis_at] // blocks).reshape((-1,) + (1,) * (len(shape) - axis_at - 1))

    gain = one(*cuts[0])
    for cut in cuts[1:]:
        gain = gain * one(*cut)
    return gain


def bell_draw(stream_key, dims, spread, most, cuts=(), dtype=jnp.bfloat16):
    result = jax.random.normal(stream_key, dims, jnp.float32) * spread
    if len(cuts) > 0:
        result = level_of(stream_key, dims, cuts, -0.22, 0.18) * result
    return jnp.clip(result, min=-most, max=most).astype(dtype)


def setup_inputs(seed: int = 0) -> dict:
    arg_keys = jax.random.split(jax.random.key(seed), 7)
    amplitudes = bell_draw(arg_keys[0], (NOCC, NOCC, NVIR, NVIR), 1.0, 6.0, ((0, 8), (1, 8), (2, 8)), jnp.float32)
    ladder_ints = bell_draw(arg_keys[1], (NVIR, NVIR, SLAB), (NVIR * NVIR) ** -0.5, 0.01171875, ((0, 8), (1, 64)), jnp.float32)
    cycle_ints = bell_draw(arg_keys[2], (NOCC, NVIR, CYCLE_SLAB), (NOCC * NVIR // 8) ** -0.5, 0.125, ((1, 64),), jnp.float32)
    occ_irrep = place_ends(jax.random.randint(arg_keys[3], (NOCC,), 0, 8), jax.random.fold_in(arg_keys[3], 1), 0, 7).astype(jnp.int32)
    vir_irrep = place_ends(jax.random.randint(arg_keys[4], (NVIR,), 0, 8), jax.random.fold_in(arg_keys[4], 1), 0, 7).astype(jnp.int32)
    pair_irrep = place_ends(jax.random.randint(arg_keys[5], (CYCLE_SLAB,), 0, 8), jax.random.fold_in(arg_keys[5], 1), 0, 7).astype(jnp.int32)
    return dict(amplitudes=amplitudes, ladder_ints=ladder_ints, cycle_ints=cycle_ints, occ_irrep=occ_irrep, vir_irrep=vir_irrep, pair_irrep=pair_irrep)


def reference(amplitudes, ladder_ints, cycle_ints, occ_irrep, vir_irrep, pair_irrep):
    highest = lax.Precision.HIGHEST
    ladder_resid = jnp.dot(amplitudes.reshape(NOCC * NOCC, NVIR * NVIR), ladder_ints.reshape(NVIR * NVIR, SLAB), precision=highest, preferred_element_type=jnp.float32)
    allowed = jnp.bitwise_xor(occ_irrep[:, None, None], vir_irrep[None, :, None]) == pair_irrep[None, None, :]
    masked = jnp.where(allowed, cycle_ints, jnp.zeros_like(cycle_ints))
    cycle_resid = jnp.einsum("ikac,kcf->iaf", amplitudes, masked, precision=highest, preferred_element_type=jnp.float32)
    return ladder_resid, cycle_resid
```

```python
import jax
import jax.numpy as jnp
from jax import lax
from jax.experimental import pallas as pl
from jax.experimental.pallas import tpu as pltpu
from jax.sharding import Mesh, PartitionSpec as P

F32 = jnp.float32
BF16 = jnp.bfloat16
VMEM_LIMIT = 16 * 1024 * 1024


def split(v):
    hi = v.astype(BF16)
    lo = (v - hi.astype(F32)).astype(BF16)
    return hi, lo


def dot3(xh, xl, bh, bl):
    def mm(p, q):
        return jnp.dot(p, q, preferred_element_type=F32)

    return mm(xh, bh) + (mm(xh, bl) + mm(xl, bh))


def regroup_kernel(a_ref, o_ref):
    rows = a_ref.reshape(512, 128)
    lane = lax.broadcasted_iota(jnp.int32, (8, 128), 1)
    low = lane < 64
    even = (lane & 32) == 0

    def swap(keep, p, q, width):
        return (
            jnp.where(keep, p, pltpu.roll(q, width, 1)),
            jnp.where(keep, pltpu.roll(p, 128 - width, 1), q),
        )

    for q in range(16):
        v = [rows[pl.ds(4 * q + c, 8, stride=64), :] for c in range(4)]
        t0, t2 = swap(low, v[0], v[2], 64)
        t1, t3 = swap(low, v[1], v[3], 64)
        o0, o1 = swap(even, t0, t1, 32)
        o2, o3 = swap(even, t2, t3, 32)
        for g, o in enumerate((o0, o1, o2, o3)):
            o_ref[g, :, pl.ds(q * 128, 128)] = o


def regroup(amplitudes):
    a = amplitudes.reshape(4, 2, 2, 64, 512)
    return pl.pallas_call(
        regroup_kernel,
        grid=(4, 2),
        in_specs=[pl.BlockSpec((4, None, 2, 64, 128), lambda b, h: (0, h, 0, 0, b))],
        out_specs=pl.BlockSpec((4, None, 8, 2048), lambda b, h: (b, h, 0, 0)),
        out_shape=jax.ShapeDtypeStruct((16, 2, 8, 2048), F32),
        compiler_params=pltpu.CompilerParams(vmem_limit_bytes=VMEM_LIMIT),
        cost_estimate=pl.CostEstimate(flops=2**20, bytes_accessed=2**22, transcendentals=0),
    )(a)


def ladder_kernel(x_ref, b0, b1, b3, near, far, o_ref, held):
    me = lax.axis_index("x")
    for k in range(8):
        part = pl.ds(k * 8, 8)
        held[me] = b0[part]
        held[lax.rem(me + 1, 4)] = b3[part]
        held[lax.rem(me + 2, 4)] = (near if k < 4 else far)[pl.ds(k % 4 * 8, 8)]
        held[lax.rem(me + 3, 4)] = b1[part]
        lanes = pl.ds(k * 256, 256)
        x = jnp.concatenate([x_ref[:, h, :, lanes].reshape(128, 256) for h in range(2)], axis=0)
        xh, xl = split(x)
        b = jnp.concatenate([held[o, c] for c in range(8) for o in range(4)], axis=0)
        bh, bl = split(b)
        total = dot3(xh, xl, bh, bl).reshape(2, 128, 640)
        if k == 0:
            o_ref[...] = total
        else:
            o_ref[...] += total


def ladder(x, *blocks):
    return pl.pallas_call(
        ladder_kernel,
        in_specs=[pl.BlockSpec(memory_space=pltpu.VMEM)] * 6,
        out_specs=pl.BlockSpec(memory_space=pltpu.VMEM),
        out_shape=jax.ShapeDtypeStruct((2, 128, 640), F32),
        scratch_shapes=[pltpu.VMEM((4, 8, 8, 640), F32)],
        compiler_params=pltpu.CompilerParams(vmem_limit_bytes=VMEM_LIMIT),
        cost_estimate=pl.CostEstimate(
            flops=3 * 2 * 256 * 2048 * 640, bytes_accessed=8 * 2**20, transcendentals=0
        ),
    )(x, *blocks)


def cycle_kernel(occ_ref, a_ref, own_ref, other_ref, vir_ref, pair_ref, o_ref, turned):
    first = (lax.axis_index("zl") * 4 + lax.axis_index("x")) * 4
    core = lax.axis_index("core")
    total = jnp.zeros((256, 128), F32)
    for s, (half, w_ref) in enumerate(((core, own_ref), (1 - core, other_ref)) * 2):
        k = 2 * half + s // 2
        allowed = jnp.bitwise_xor(vir_ref[...], occ_ref[first + k]) == pair_ref[...]
        w = jnp.where(allowed, w_ref[:, s // 2].reshape(512, 128), 0.0)
        ah, al = split(a_ref[:, k].reshape(256, 512))
        wh, wl = split(w)
        total = total + dot3(ah, al, wh, wl)
    turned[...] = total.T
    for x in range(4):
        for d in range(16):
            o_ref[x, pl.ds(2 * d, 2), :] = turned[pl.ds(8 * d + 2 * x, 2), :]


def cycle(occ, amplitudes, own, other, vir, pair):
    return pl.pallas_call(
        cycle_kernel,
        in_specs=[pl.BlockSpec(memory_space=pltpu.SMEM)]
        + [pl.BlockSpec(memory_space=pltpu.VMEM)] * 5,
        out_specs=pl.BlockSpec(memory_space=pltpu.VMEM),
        out_shape=jax.ShapeDtypeStruct((4, 32, 256), F32),
        scratch_shapes=[pltpu.VMEM((128, 256), F32)],
        compiler_params=pltpu.CompilerParams(vmem_limit_bytes=VMEM_LIMIT),
        cost_estimate=pl.CostEstimate(
            flops=3 * 2 * 256 * 2048 * 128, bytes_accessed=3 * 2**20, transcendentals=0
        ),
    )(occ, amplitudes, own, other, vir, pair)


def pack_kernel(part_ref, c0, c1, c2, c3, o_ref, ladder_sum, cycle_sum):
    ladder_sum[...] = part_ref[0] + part_ref[1]
    cycle_sum[...] = (c0[...] + c1[...]) + (c2[...] + c3[...])
    for d in range(64):
        o_ref[d, :, pl.ds(0, 640)] = ladder_sum[pl.ds(2 * d, 2), :]
        o_ref[d, :, pl.ds(640, 256)] = cycle_sum[pl.ds(d // 4 * 2, 2), :]


def pack(part, parts):
    return pl.pallas_call(
        pack_kernel,
        out_shape=jax.ShapeDtypeStruct((64, 2, 896), F32),
        scratch_shapes=[pltpu.VMEM((128, 640), F32), pltpu.VMEM((32, 256), F32)],
        compiler_params=pltpu.CompilerParams(vmem_limit_bytes=VMEM_LIMIT),
        cost_estimate=pl.CostEstimate(flops=2**18, bytes_accessed=2**20, transcendentals=0),
    )(part, *parts)


def finish_kernel(p_ref, ladder_ref, cycle_ref):
    zh = lax.axis_index("zh")
    total = [p_ref[d, :, pl.ds(0, 640)] for d in range(8)]
    for d in range(8, 64):
        total[d % 8] += p_ref[d, :, pl.ds(0, 640)]
    while len(total) > 1:
        total = [p + q for p, q in zip(total[::2], total[1::2])]
    ladder_ref[...] = total[0]
    for y in range(8):
        cycle_ref[y] = (
            p_ref[y * 8 + zh, :, pl.ds(640, 256)] + p_ref[y * 8 + 4 + zh, :, pl.ds(640, 256)]
        )


def finish(p):
    return pl.pallas_call(
        finish_kernel,
        out_shape=[
            jax.ShapeDtypeStruct((2, 640), F32),
            jax.ShapeDtypeStruct((8, 2, 256), F32),
        ],
        compiler_params=pltpu.CompilerParams(vmem_limit_bytes=VMEM_LIMIT),
        cost_estimate=pl.CostEstimate(flops=2**17, bytes_accessed=2**19, transcendentals=0),
    )(p)


def exchange(v, axes):
    return lax.all_to_all(v, axes, split_axis=0, concat_axis=0, tiled=True)


def body(amplitudes, ladder_ints, cycle_ints, occ_irrep, vir_irrep, pair_irrep):
    w = exchange(cycle_ints.reshape(8, 4, 8, 128), ("zl", "x"))

    ring = [[(i, (i + s) % 4) for i in range(4)] for s in range(4)]
    sent = regroup(amplitudes)
    x = exchange(sent, ("y", "zl"))
    w = lax.dynamic_index_in_dim(
        w.reshape(8, 2, 2, 8, 128), lax.axis_index("core"), axis=1, keepdims=False
    )
    w = lax.all_gather(w, "y", axis=0, tiled=True)
    other = lax.ppermute(w, "core", [(0, 1), (1, 0)])
    _, ladder_ints, vir_irrep = lax.optimization_barrier((sent, ladder_ints, vir_irrep))
    b1 = lax.ppermute(ladder_ints, "x", ring[1])
    b3 = lax.ppermute(ladder_ints, "x", ring[3])
    from_b1, from_b3, w = lax.optimization_barrier((b1, b3, w))
    near = lax.ppermute(from_b1[:32], "x", ring[1])
    far = lax.ppermute(from_b3[32:], "x", ring[3])

    vir = jnp.broadcast_to(vir_irrep[:, None], (512, 128))
    parts = cycle(occ_irrep, amplitudes, w, other, vir, pair_irrep[None])
    at = lax.axis_index("x")
    parts = [
        lax.dynamic_index_in_dim(parts, lax.rem(at + s, 4), keepdims=False) for s in range(4)
    ]
    parts = parts[:1] + [lax.ppermute(parts[s], "x", ring[s]) for s in (1, 2, 3)]

    part = exchange(ladder(x, ladder_ints, b1, b3, near, far), ("core",))
    part, cycle_part = finish(exchange(pack(part, parts), ("y", "zl", "zh")))
    cycle_resid = cycle_part.reshape(8, 2, 4, 64).transpose(0, 2, 3, 1).reshape(32, 64, 2)
    move = [
        ((s * 4 + a) * 4 + hi * 2 + lo, (hi * 4 + lo * 2 + s) * 4 + a)
        for s in range(2)
        for a in range(4)
        for hi in range(2)
        for lo in range(2)
    ]
    ladder_resid = lax.ppermute(part, ("zl", "x", "zh"), move)
    return ladder_resid, cycle_resid


def solution(mesh):
    fine = Mesh(mesh.devices.reshape(8, 2, 4, 4, 2), ("y", "zl", "x", "zh", "core"))
    col, depth = ("zl", "x"), ("zh", "core")
    in_specs = (
        P("y", col, depth, None),
        P(depth, ("y", "zl", "x"), None),
        P(None, ("y", "zl", "x"), None),
        P(),
        P(),
        P(),
    )
    out_specs = (P(("y", "zl", "x", "zh", "core"), None), P(None, depth, ("y", "zl", "x")))
    return jax.shard_map(body, mesh=fine, in_specs=in_specs, out_specs=out_specs, check_vma=False)
```

```python
import jax
import jax.numpy as jnp
from jax import lax
from jax.experimental import pallas as pl
from jax.experimental.pallas import tpu as pltpu
from jax.sharding import Mesh, PartitionSpec as P

F32 = jnp.float32
BF16 = jnp.bfloat16
VMEM_LIMIT = 16 * 1024 * 1024


def split(v):
    hi = v.astype(BF16)
    lo = (v - hi.astype(F32)).astype(BF16)
    return hi, lo


def dot3(xh, xl, bh, bl):
    def mm(p, q):
        return jnp.dot(p, q, preferred_element_type=F32)

    return mm(xh, bh) + (mm(xh, bl) + mm(xl, bh))


def regroup_kernel(a_ref, o_ref):
    rows = a_ref.reshape(512, 128)
    lane = lax.broadcasted_iota(jnp.int32, (8, 128), 1)
    low = lane < 64
    even = (lane & 32) == 0

    def swap(keep, p, q, width):
        return (
            jnp.where(keep, p, pltpu.roll(q, width, 1)),
            jnp.where(keep, pltpu.roll(p, 128 - width, 1), q),
        )

    for q in range(16):
        v = [rows[pl.ds(4 * q + c, 8, stride=64), :] for c in range(4)]
        t0, t2 = swap(low, v[0], v[2], 64)
        t1, t3 = swap(low, v[1], v[3], 64)
        o0, o1 = swap(even, t0, t1, 32)
        o2, o3 = swap(even, t2, t3, 32)
        for g, o in enumerate((o0, o1, o2, o3)):
            o_ref[g, :, pl.ds(q * 128, 128)] = o


def regroup(amplitudes):
    a = amplitudes.reshape(4, 2, 2, 64, 512)
    return pl.pallas_call(
        regroup_kernel,
        grid=(4, 2),
        in_specs=[pl.BlockSpec((4, None, 2, 64, 128), lambda b, h: (0, h, 0, 0, b))],
        out_specs=pl.BlockSpec((4, None, 8, 2048), lambda b, h: (b, h, 0, 0)),
        out_shape=jax.ShapeDtypeStruct((16, 2, 8, 2048), F32),
        compiler_params=pltpu.CompilerParams(vmem_limit_bytes=VMEM_LIMIT),
        cost_estimate=pl.CostEstimate(flops=2**20, bytes_accessed=2**22, transcendentals=0),
    )(a)


def ladder_kernel(x_ref, b1, b3, b0, near, far, o_ref, held, sems):
    me = lax.axis_index("x")

    def copies(k):
        part = pl.ds(k * 16, 16)
        across = (near if k < 2 else far).at[pl.ds(k % 2 * 16, 16)]
        return (
            pltpu.make_async_copy(b0.at[part], held.at[me, part], sems.at[0, k]),
            pltpu.make_async_copy(across, held.at[lax.rem(me + 2, 4), part], sems.at[1, k]),
        )

    for k in range(4):
        for copy in copies(k):
            copy.start()
    for k in range(4):
        part = pl.ds(k * 16, 16)
        held[lax.rem(me + 1, 4), part] = b3[part]
        held[lax.rem(me + 3, 4), part] = b1[part]
        span = pl.ds(k * 512, 512)
        x = jnp.concatenate([x_ref[:, h, :, span].reshape(128, 512) for h in range(2)], axis=0)
        xh, xl = split(x)
        for copy in copies(k):
            copy.wait()
        b = [held[o, k * 16 + c] for c in range(16) for o in range(4)]
        bh, bl = split(jnp.concatenate(b, axis=0))
        total = dot3(xh, xl, bh, bl).reshape(2, 128, 640)
        if k == 0:
            o_ref[...] = total
        else:
            o_ref[...] += total


VMEM = pl.BlockSpec(memory_space=pltpu.VMEM)


def small(kernel, out_shape, *args, scratch=()):
    return pl.pallas_call(
        kernel,
        in_specs=[VMEM] * len(args),
        out_specs=VMEM if isinstance(out_shape, tuple) else [VMEM] * len(out_shape),
        out_shape=jax.ShapeDtypeStruct(out_shape, F32)
        if isinstance(out_shape, tuple)
        else [jax.ShapeDtypeStruct(shape, F32) for shape in out_shape],
        scratch_shapes=[pltpu.VMEM(shape, F32) for shape in scratch],
        compiler_params=pltpu.CompilerParams(vmem_limit_bytes=VMEM_LIMIT),
        cost_estimate=pl.CostEstimate(flops=2**18, bytes_accessed=2**20, transcendentals=0),
    )(*args)


def ladder(x, b0, b1, b3, near, far):
    anywhere = pl.BlockSpec(memory_space=pl.ANY)
    return pl.pallas_call(
        ladder_kernel,
        in_specs=[VMEM] * 3 + [anywhere] * 3,
        out_specs=VMEM,
        out_shape=jax.ShapeDtypeStruct((2, 128, 640), F32),
        scratch_shapes=[pltpu.VMEM((4, 64, 8, 640), F32), pltpu.SemaphoreType.DMA((2, 4))],
        compiler_params=pltpu.CompilerParams(vmem_limit_bytes=50 * 1024 * 1024),
        cost_estimate=pl.CostEstimate(
            flops=3 * 2 * 256 * 2048 * 640, bytes_accessed=8 * 2**20, transcendentals=0
        ),
    )(x, b1, b3, b0, near, far)


def cores_kernel(p_ref, o_ref, total):
    total[...] = p_ref[0] + p_ref[1]
    for y in range(8):
        for d in range(8):
            o_ref[d, y] = total[pl.ds(16 * y + 2 * d, 2), :]


def depth_kernel(p_ref, o_ref):
    for y in range(8):
        p = [p_ref[s, y] for s in range(8)]
        o_ref[y] = ((p[0] + p[1]) + (p[2] + p[3])) + ((p[4] + p[5]) + (p[6] + p[7]))


def pack_kernel(l_ref, c_ref, o_ref):
    for y in range(8):
        p = [c_ref[s, y] for s in range(8)]
        o_ref[y, :, pl.ds(0, 640)] = l_ref[y]
        o_ref[y, :, pl.ds(640, 256)] = ((p[0] + p[1]) + (p[2] + p[3])) + (
            (p[4] + p[5]) + (p[6] + p[7])
        )


def finish_kernel(p_ref, ladder_ref, cycle_ref):
    p = [p_ref[y, :, pl.ds(0, 640)] for y in range(8)]
    ladder_ref[...] = ((p[0] + p[1]) + (p[2] + p[3])) + ((p[4] + p[5]) + (p[6] + p[7]))
    cycle_ref[...] = p_ref[:, :, pl.ds(640, 256)]


def cycle_kernel(occ_ref, a_ref, w_ref, vir_ref, pair_ref, o_ref, turned):
    first = (lax.axis_index("zl") * 4 + lax.axis_index("x")) * 4
    total = jnp.zeros((256, 128), F32)
    for k in range(4):
        allowed = jnp.bitwise_xor(vir_ref[...], occ_ref[first + k]) == pair_ref[...]
        w = jnp.where(allowed, w_ref[:, k].reshape(512, 128), 0.0)
        ah, al = split(a_ref[:, k].reshape(256, 512))
        wh, wl = split(w)
        total = total + dot3(ah, al, wh, wl)
    turned[...] = total.T
    for col in range(8):
        for y in range(8):
            o_ref[col, y] = turned[pl.ds(16 * y + 2 * col, 2), :]


def cycle(occ, amplitudes, w, vir, pair):
    return pl.pallas_call(
        cycle_kernel,
        in_specs=[pl.BlockSpec(memory_space=pltpu.SMEM)] + [VMEM] * 4,
        out_specs=VMEM,
        out_shape=jax.ShapeDtypeStruct((8, 8, 2, 256), F32),
        scratch_shapes=[pltpu.VMEM((128, 256), F32)],
        compiler_params=pltpu.CompilerParams(vmem_limit_bytes=VMEM_LIMIT),
        cost_estimate=pl.CostEstimate(
            flops=3 * 2 * 256 * 2048 * 128, bytes_accessed=3 * 2**20, transcendentals=0
        ),
    )(occ, amplitudes, w, vir, pair)


def exchange(v, axes):
    return lax.all_to_all(v, axes, split_axis=0, concat_axis=0, tiled=True)


def body(amplitudes, ladder_ints, cycle_ints, occ_irrep, vir_irrep, pair_irrep):
    w = exchange(cycle_ints.reshape(8, 4, 8, 128), ("zl", "x"))

    ring = [[(i, (i + s) % 4) for i in range(4)] for s in range(4)]
    sent = regroup(amplitudes)
    x = exchange(sent, ("y", "zl"))
    w = lax.all_gather(w, "y", axis=0, tiled=True)
    _, ladder_ints, vir_irrep = lax.optimization_barrier((sent, ladder_ints, vir_irrep))
    b1 = lax.ppermute(ladder_ints, "x", ring[1])
    b3 = lax.ppermute(ladder_ints, "x", ring[3])
    near = lax.ppermute(b1[:32], "x", ring[1])
    far = lax.ppermute(b3[32:], "x", ring[3])
    part = exchange(ladder(x, ladder_ints, b1, b3, near, far), ("core",))
    part = small(cores_kernel, (8, 8, 2, 640), part, scratch=[(128, 640)])

    vir = jnp.broadcast_to(vir_irrep[:, None], (512, 128))
    _, late = lax.optimization_barrier((part, w))
    cycle_part = cycle(occ_irrep, amplitudes, late, vir, pair_irrep[None])
    part = small(depth_kernel, (8, 2, 640), exchange(part, ("zl", "zh")))
    _, cycle_part = lax.optimization_barrier((part, cycle_part))
    move = [
        ((s * 4 + a) * 4 + hi * 2 + lo, (hi * 4 + lo * 2 + s) * 4 + a)
        for s in range(2)
        for a in range(4)
        for hi in range(2)
        for lo in range(2)
    ]
    part = lax.ppermute(part, ("zl", "x", "zh"), move)
    cycle_part = exchange(cycle_part, ("zl", "x"))
    both = exchange(small(pack_kernel, (8, 2, 896), part, cycle_part), ("y",))
    ladder_resid, cycle_part = small(finish_kernel, [(2, 640), (8, 2, 256)], both)
    cycle_resid = cycle_part.reshape(8, 2, 4, 64).transpose(0, 2, 3, 1).reshape(32, 64, 2)
    return ladder_resid, cycle_resid


def solution(mesh):
    fine = Mesh(mesh.devices.reshape(8, 2, 4, 4, 2), ("y", "zl", "x", "zh", "core"))
    col, depth = ("zl", "x"), ("zh", "core")
    in_specs = (
        P("y", col, depth, None),
        P(depth, ("y", "zl", "x"), None),
        P(None, ("y", "zl", "x"), None),
        P(),
        P(),
        P(),
    )
    out_specs = (P(("y", "zl", "x", "zh", "core"), None), P(None, depth, ("y", "zl", "x")))
    return jax.shard_map(body, mesh=fine, in_specs=in_specs, out_specs=out_specs, check_vma=False)
```

```python
import jax
import jax.numpy as jnp
from jax import lax
from jax.experimental import pallas as pl
from jax.experimental.pallas import tpu as pltpu
from jax.sharding import Mesh, PartitionSpec as P

F32 = jnp.float32
BF16 = jnp.bfloat16
VMEM_LIMIT = 16 * 1024 * 1024
LADDER_LIMIT = 50 * 1024 * 1024


def split(v):
    hi = v.astype(BF16)
    lo = (v - hi.astype(F32)).astype(BF16)
    return hi, lo


def dot3(xh, xl, bh, bl):
    def mm(p, q):
        return jnp.dot(p, q, preferred_element_type=F32)

    return mm(xh, bh) + (mm(xh, bl) + mm(xl, bh))


def regroup_kernel(a_ref, o_ref):
    rows = a_ref.reshape(512, 128)
    lane = lax.broadcasted_iota(jnp.int32, (8, 128), 1)
    low = lane < 64
    even = (lane & 32) == 0

    def swap(keep, p, q, width):
        return (
            jnp.where(keep, p, pltpu.roll(q, width, 1)),
            jnp.where(keep, pltpu.roll(p, 128 - width, 1), q),
        )

    for q in range(16):
        v = [rows[pl.ds(4 * q + c, 8, stride=64), :] for c in range(4)]
        t0, t2 = swap(low, v[0], v[2], 64)
        t1, t3 = swap(low, v[1], v[3], 64)
        o0, o1 = swap(even, t0, t1, 32)
        o2, o3 = swap(even, t2, t3, 32)
        for g, o in enumerate((o0, o1, o2, o3)):
            o_ref[g, :, pl.ds(q * 128, 128)] = o


def regroup(amplitudes):
    a = amplitudes.reshape(4, 2, 2, 64, 512)
    return pl.pallas_call(
        regroup_kernel,
        grid=(4, 2),
        in_specs=[pl.BlockSpec((4, None, 2, 64, 128), lambda b, h: (0, h, 0, 0, b))],
        out_specs=pl.BlockSpec((4, None, 8, 2048), lambda b, h: (b, h, 0, 0)),
        out_shape=jax.ShapeDtypeStruct((16, 2, 8, 2048), F32),
        compiler_params=pltpu.CompilerParams(vmem_limit_bytes=VMEM_LIMIT),
        cost_estimate=pl.CostEstimate(flops=2**20, bytes_accessed=2**22, transcendentals=0),
    )(a)


def ladder_kernel(x_ref, b1, b3, b0, near, far, o_ref, held, sems):
    me = lax.axis_index("x")

    def copies(k):
        part = pl.ds(k * 16, 16)
        across = (near if k < 2 else far).at[pl.ds(k % 2 * 16, 16)]
        return (
            pltpu.make_async_copy(b0.at[part], held.at[me, part], sems.at[0, k]),
            pltpu.make_async_copy(across, held.at[lax.rem(me + 2, 4), part], sems.at[1, k]),
        )

    for k in range(4):
        for copy in copies(k):
            copy.start()
    for k in range(4):
        part = pl.ds(k * 16, 16)
        held[lax.rem(me + 1, 4), part] = b3[part]
        held[lax.rem(me + 3, 4), part] = b1[part]
        span = pl.ds(k * 512, 512)
        x = jnp.concatenate([x_ref[:, h, :, span].reshape(128, 512) for h in range(2)], axis=0)
        xh, xl = split(x)
        for copy in copies(k):
            copy.wait()
        b = [held[o, k * 16 + c] for c in range(16) for o in range(4)]
        bh, bl = split(jnp.concatenate(b, axis=0))
        total = dot3(xh, xl, bh, bl).reshape(2, 128, 640)
        if k == 0:
            o_ref[...] = total
        else:
            o_ref[...] += total


VMEM = pl.BlockSpec(memory_space=pltpu.VMEM)


def small(kernel, out_shape, *args, scratch=()):
    return pl.pallas_call(
        kernel,
        in_specs=[VMEM] * len(args),
        out_specs=VMEM if isinstance(out_shape, tuple) else [VMEM] * len(out_shape),
        out_shape=jax.ShapeDtypeStruct(out_shape, F32)
        if isinstance(out_shape, tuple)
        else [jax.ShapeDtypeStruct(shape, F32) for shape in out_shape],
        scratch_shapes=[pltpu.VMEM(shape, F32) for shape in scratch],
        compiler_params=pltpu.CompilerParams(vmem_limit_bytes=VMEM_LIMIT),
        cost_estimate=pl.CostEstimate(flops=2**18, bytes_accessed=2**20, transcendentals=0),
    )(*args)


def ladder(x, b0, b1, b3, near, far):
    anywhere = pl.BlockSpec(memory_space=pl.ANY)
    return pl.pallas_call(
        ladder_kernel,
        in_specs=[VMEM] * 3 + [anywhere] * 3,
        out_specs=VMEM,
        out_shape=jax.ShapeDtypeStruct((2, 128, 640), F32),
        scratch_shapes=[pltpu.VMEM((4, 64, 8, 640), F32), pltpu.SemaphoreType.DMA((2, 4))],
        compiler_params=pltpu.CompilerParams(vmem_limit_bytes=LADDER_LIMIT),
        cost_estimate=pl.CostEstimate(
            flops=3 * 2 * 256 * 2048 * 640, bytes_accessed=8 * 2**20, transcendentals=0
        ),
    )(x, b1, b3, b0, near, far)


def spread_kernel(w_ref, o_ref):
    core = lax.axis_index("core")
    for col in range(8):
        for y in range(8):
            o_ref[y * 8 + col] = w_ref[pl.ds(col * 4 + 2 * core, 2)]


def pack_kernel(part_ref, c0, c1, c2, c3, o_ref, ladder_sum, cycle_sum):
    ladder_sum[...] = part_ref[0] + part_ref[1]
    cycle_sum[...] = (c0[...] + c1[...]) + (c2[...] + c3[...])
    for d in range(64):
        o_ref[d, :, pl.ds(0, 640)] = ladder_sum[pl.ds(2 * d, 2), :]
        o_ref[d, :, pl.ds(640, 256)] = cycle_sum[pl.ds(d // 4 * 2, 2), :]


def finish_kernel(p_ref, ladder_ref, cycle_ref):
    zh = lax.axis_index("zh")
    total = [p_ref[d, :, pl.ds(0, 640)] for d in range(8)]
    for d in range(8, 64):
        total[d % 8] += p_ref[d, :, pl.ds(0, 640)]
    while len(total) > 1:
        total = [p + q for p, q in zip(total[::2], total[1::2])]
    ladder_ref[...] = total[0]
    for y in range(8):
        cycle_ref[y] = (
            p_ref[y * 8 + zh, :, pl.ds(640, 256)] + p_ref[y * 8 + 4 + zh, :, pl.ds(640, 256)]
        )


def cycle_kernel(occ_ref, a_ref, own_ref, other_ref, vir_ref, pair_ref, o_ref, turned):
    first = (lax.axis_index("zl") * 4 + lax.axis_index("x")) * 4
    core = lax.axis_index("core")
    total = jnp.zeros((256, 128), F32)
    for half, w_ref in ((core, own_ref), (1 - core, other_ref)):
        for s in range(2):
            k = 2 * half + s
            allowed = jnp.bitwise_xor(vir_ref[...], occ_ref[first + k]) == pair_ref[...]
            w = jnp.where(allowed, w_ref[:, s].reshape(512, 128), 0.0)
            ah, al = split(a_ref[:, k].reshape(256, 512))
            wh, wl = split(w)
            total = total + dot3(ah, al, wh, wl)
    turned[...] = total.T
    for x in range(4):
        to = lax.rem(x + 4 - lax.axis_index("x"), 4)
        for d in range(16):
            o_ref[to, pl.ds(2 * d, 2), :] = turned[pl.ds(8 * d + 2 * x, 2), :]


def cycle(occ, amplitudes, own, other, vir, pair):
    return pl.pallas_call(
        cycle_kernel,
        in_specs=[pl.BlockSpec(memory_space=pltpu.SMEM)] + [VMEM] * 5,
        out_specs=VMEM,
        out_shape=jax.ShapeDtypeStruct((4, 32, 256), F32),
        scratch_shapes=[pltpu.VMEM((128, 256), F32)],
        compiler_params=pltpu.CompilerParams(vmem_limit_bytes=VMEM_LIMIT),
        cost_estimate=pl.CostEstimate(
            flops=3 * 2 * 256 * 2048 * 128, bytes_accessed=3 * 2**20, transcendentals=0
        ),
    )(occ, amplitudes, own, other, vir, pair)


def exchange(v, axes):
    return lax.all_to_all(v, axes, split_axis=0, concat_axis=0, tiled=True)


def body(amplitudes, ladder_ints, cycle_ints, occ_irrep, vir_irrep, pair_irrep):
    own = exchange(small(spread_kernel, (64, 2, 8, 128), cycle_ints), ("y", "zl", "x"))

    ring = [[(i, (i + s) % 4) for i in range(4)] for s in range(4)]
    sent = regroup(amplitudes)
    _, ladder_ints = lax.optimization_barrier((sent, ladder_ints))
    sent, own = lax.optimization_barrier((sent, own))
    x = exchange(sent, ("y", "zl"))
    other = lax.ppermute(own, "core", [(0, 1), (1, 0)])
    b1 = lax.ppermute(ladder_ints, "x", ring[1])
    b3 = lax.ppermute(ladder_ints, "x", ring[3])
    near = lax.ppermute(b1[:32], "x", ring[1])
    far = lax.ppermute(b3[32:], "x", ring[3])

    vir = jnp.broadcast_to(vir_irrep[:, None], (512, 128))
    parts = cycle(occ_irrep, amplitudes, own, other, vir, pair_irrep[None])
    parts = [parts[0]] + [lax.ppermute(parts[s], "x", ring[s]) for s in (1, 2, 3)]

    part = exchange(ladder(x, ladder_ints, b1, b3, near, far), ("core",))
    both = small(pack_kernel, (64, 2, 896), part, *parts, scratch=[(128, 640), (32, 256)])
    both = exchange(both, ("y", "zl", "zh"))
    part, cycle_part = small(finish_kernel, [(2, 640), (8, 2, 256)], both)
    cycle_resid = cycle_part.reshape(8, 2, 4, 64).transpose(0, 2, 3, 1).reshape(32, 64, 2)
    move = [
        ((s * 4 + a) * 4 + hi * 2 + lo, (hi * 4 + lo * 2 + s) * 4 + a)
        for s in range(2)
        for a in range(4)
        for hi in range(2)
        for lo in range(2)
    ]
    ladder_resid = lax.ppermute(part, ("zl", "x", "zh"), move)
    return ladder_resid, cycle_resid


def solution(mesh):
    fine = Mesh(mesh.devices.reshape(8, 2, 4, 4, 2), ("y", "zl", "x", "zh", "core"))
    col, depth = ("zl", "x"), ("zh", "core")
    in_specs = (
        P("y", col, depth, None),
        P(depth, ("y", "zl", "x"), None),
        P(None, ("y", "zl", "x"), None),
        P(),
        P(),
        P(),
    )
    out_specs = (P(("y", "zl", "x", "zh", "core"), None), P(None, depth, ("y", "zl", "x")))
    return jax.shard_map(body, mesh=fine, in_specs=in_specs, out_specs=out_specs, check_vma=False)
```

```python
import jax
import jax.numpy as jnp
from jax import lax
from jax.experimental import pallas as pl
from jax.experimental.pallas import tpu as pltpu
from jax.sharding import Mesh, PartitionSpec as P

F32 = jnp.float32
BF16 = jnp.bfloat16
VMEM_LIMIT = 16 * 1024 * 1024
LADDER_LIMIT = 50 * 1024 * 1024


def split(v):
    hi = v.astype(BF16)
    lo = (v - hi.astype(F32)).astype(BF16)
    return hi, lo


def dot3(xh, xl, bh, bl):
    def mm(p, q):
        return jnp.dot(p, q, preferred_element_type=F32)

    return mm(xh, bh) + (mm(xh, bl) + mm(xl, bh))


def regroup_kernel(a_ref, o_ref):
    rows = a_ref.reshape(512, 128)
    lane = lax.broadcasted_iota(jnp.int32, (8, 128), 1)
    low = lane < 64
    even = (lane & 32) == 0

    def swap(keep, p, q, width):
        return (
            jnp.where(keep, p, pltpu.roll(q, width, 1)),
            jnp.where(keep, pltpu.roll(p, 128 - width, 1), q),
        )

    for q in range(16):
        v = [rows[pl.ds(4 * q + c, 8, stride=64), :] for c in range(4)]
        t0, t2 = swap(low, v[0], v[2], 64)
        t1, t3 = swap(low, v[1], v[3], 64)
        o0, o1 = swap(even, t0, t1, 32)
        o2, o3 = swap(even, t2, t3, 32)
        for g, o in enumerate((o0, o1, o2, o3)):
            o_ref[g, :, pl.ds(q * 128, 128)] = o


def regroup(amplitudes):
    a = amplitudes.reshape(4, 2, 2, 64, 512)
    return pl.pallas_call(
        regroup_kernel,
        grid=(4, 2),
        in_specs=[pl.BlockSpec((4, None, 2, 64, 128), lambda b, h: (0, h, 0, 0, b))],
        out_specs=pl.BlockSpec((4, None, 8, 2048), lambda b, h: (b, h, 0, 0)),
        out_shape=jax.ShapeDtypeStruct((16, 2, 8, 2048), F32),
        compiler_params=pltpu.CompilerParams(vmem_limit_bytes=VMEM_LIMIT),
        cost_estimate=pl.CostEstimate(flops=2**20, bytes_accessed=2**22, transcendentals=0),
    )(a)


def ladder_kernel(x_ref, b1, b3, b0, near, far, o_ref, held, sems):
    me = lax.axis_index("x")

    def copies(k):
        part = pl.ds(k * 16, 16)
        across = (near if k < 2 else far).at[pl.ds(k % 2 * 16, 16)]
        return (
            pltpu.make_async_copy(b0.at[part], held.at[me, part], sems.at[0, k]),
            pltpu.make_async_copy(across, held.at[lax.rem(me + 2, 4), part], sems.at[1, k]),
        )

    for k in range(4):
        for copy in copies(k):
            copy.start()
    for k in range(4):
        part = pl.ds(k * 16, 16)
        held[lax.rem(me + 1, 4), part] = b3[part]
        held[lax.rem(me + 3, 4), part] = b1[part]
        span = pl.ds(k * 512, 512)
        x = jnp.concatenate([x_ref[:, h, :, span].reshape(128, 512) for h in range(2)], axis=0)
        xh, xl = split(x)
        for copy in copies(k):
            copy.wait()
        b = [held[o, k * 16 + c] for c in range(16) for o in range(4)]
        bh, bl = split(jnp.concatenate(b, axis=0))
        total = dot3(xh, xl, bh, bl).reshape(2, 128, 640)
        if k == 0:
            o_ref[...] = total
        else:
            o_ref[...] += total


VMEM = pl.BlockSpec(memory_space=pltpu.VMEM)


def small(kernel, out_shape, *args, scratch=()):
    return pl.pallas_call(
        kernel,
        in_specs=[VMEM] * len(args),
        out_specs=VMEM if isinstance(out_shape, tuple) else [VMEM] * len(out_shape),
        out_shape=jax.ShapeDtypeStruct(out_shape, F32)
        if isinstance(out_shape, tuple)
        else [jax.ShapeDtypeStruct(shape, F32) for shape in out_shape],
        scratch_shapes=[pltpu.VMEM(shape, F32) for shape in scratch],
        compiler_params=pltpu.CompilerParams(vmem_limit_bytes=VMEM_LIMIT),
        cost_estimate=pl.CostEstimate(flops=2**18, bytes_accessed=2**20, transcendentals=0),
    )(*args)


def ladder(x, b0, b1, b3, near, far):
    anywhere = pl.BlockSpec(memory_space=pl.ANY)
    return pl.pallas_call(
        ladder_kernel,
        in_specs=[VMEM] * 3 + [anywhere] * 3,
        out_specs=VMEM,
        out_shape=jax.ShapeDtypeStruct((2, 128, 640), F32),
        scratch_shapes=[pltpu.VMEM((4, 64, 8, 640), F32), pltpu.SemaphoreType.DMA((2, 4))],
        compiler_params=pltpu.CompilerParams(vmem_limit_bytes=LADDER_LIMIT),
        cost_estimate=pl.CostEstimate(
            flops=3 * 2 * 256 * 2048 * 640, bytes_accessed=8 * 2**20, transcendentals=0
        ),
    )(x, b1, b3, b0, near, far)


def spread_kernel(w_ref, o_ref):
    zh = lax.axis_index("zh")
    for col in range(8):
        for y in range(8):
            o_ref[y * 8 + col] = w_ref[col * 4 + zh]


def pack_kernel(part_ref, c0, c1, c2, c3, o_ref, ladder_sum, cycle_sum):
    ladder_sum[...] = part_ref[0] + part_ref[1]
    cycle_sum[...] = (c0[...] + c1[...]) + (c2[...] + c3[...])
    for d in range(64):
        o_ref[d, :, pl.ds(0, 640)] = ladder_sum[pl.ds(2 * d, 2), :]
        o_ref[d, :, pl.ds(640, 256)] = cycle_sum[pl.ds(d // 4 * 2, 2), :]


def finish_kernel(p_ref, ladder_ref, cycle_ref):
    zh = lax.axis_index("zh")
    total = [p_ref[d, :, pl.ds(0, 640)] for d in range(8)]
    for d in range(8, 64):
        total[d % 8] += p_ref[d, :, pl.ds(0, 640)]
    while len(total) > 1:
        total = [p + q for p, q in zip(total[::2], total[1::2])]
    ladder_ref[...] = total[0]
    for y in range(8):
        cycle_ref[y] = (
            p_ref[y * 8 + zh, :, pl.ds(640, 256)] + p_ref[y * 8 + 4 + zh, :, pl.ds(640, 256)]
        )


def cycle_kernel(occ_ref, a_ref, w0, w1, w2, w3, vir_ref, pair_ref, o_ref, turned):
    first = (lax.axis_index("zl") * 4 + lax.axis_index("x")) * 4
    total = jnp.zeros((256, 128), F32)
    for s, w_ref in enumerate((w0, w1, w2, w3)):
        k = lax.rem(lax.axis_index("zh") + 4 - s, 4)
        allowed = jnp.bitwise_xor(vir_ref[...], occ_ref[first + k]) == pair_ref[...]
        w = jnp.where(allowed, w_ref[...].reshape(512, 128), 0.0)
        ah, al = split(a_ref[:, k].reshape(256, 512))
        wh, wl = split(w)
        total = total + dot3(ah, al, wh, wl)
    turned[...] = total.T
    for x in range(4):
        to = lax.rem(x + 4 - lax.axis_index("x"), 4)
        for d in range(16):
            o_ref[to, pl.ds(2 * d, 2), :] = turned[pl.ds(8 * d + 2 * x, 2), :]


def cycle(occ, amplitudes, w, vir, pair):
    return pl.pallas_call(
        cycle_kernel,
        in_specs=[pl.BlockSpec(memory_space=pltpu.SMEM)] + [VMEM] * 7,
        out_specs=VMEM,
        out_shape=jax.ShapeDtypeStruct((4, 32, 256), F32),
        scratch_shapes=[pltpu.VMEM((128, 256), F32)],
        compiler_params=pltpu.CompilerParams(vmem_limit_bytes=VMEM_LIMIT),
        cost_estimate=pl.CostEstimate(
            flops=3 * 2 * 256 * 2048 * 128, bytes_accessed=3 * 2**20, transcendentals=0
        ),
    )(occ, amplitudes, *w, vir, pair)


def exchange(v, axes):
    return lax.all_to_all(v, axes, split_axis=0, concat_axis=0, tiled=True)


def body(amplitudes, ladder_ints, cycle_ints, occ_irrep, vir_irrep, pair_irrep):
    w = exchange(small(spread_kernel, (64, 8, 128), cycle_ints), ("y", "zl", "x"))

    ring = [[(i, (i + s) % 4) for i in range(4)] for s in range(4)]
    sent = regroup(amplitudes)
    _, ladder_ints = lax.optimization_barrier((sent, ladder_ints))
    sent, w = lax.optimization_barrier((sent, w))
    x = exchange(sent, ("y", "zl"))
    b1 = lax.ppermute(ladder_ints, "x", ring[1])
    b3 = lax.ppermute(ladder_ints, "x", ring[3])
    w = [w] + [lax.ppermute(w, "zh", ring[s]) for s in (1, 2, 3)]
    from_b1, from_b3, *w = lax.optimization_barrier((b1, b3, *w))
    near = lax.ppermute(from_b1[:32], "x", ring[1])
    far = lax.ppermute(from_b3[32:], "x", ring[3])

    vir = jnp.broadcast_to(vir_irrep[:, None], (512, 128))
    parts = cycle(occ_irrep, amplitudes, w, vir, pair_irrep[None])
    parts = [parts[0]] + [lax.ppermute(parts[s], "x", ring[s]) for s in (1, 2, 3)]

    part = ladder(x, ladder_ints, b1, b3, near, far)
    part = exchange(part, ("core",))
    both = small(pack_kernel, (64, 2, 896), part, *parts, scratch=[(128, 640), (32, 256)])
    both = exchange(both, ("y", "zl", "zh"))
    part, cycle_part = small(finish_kernel, [(2, 640), (8, 2, 256)], both)
    cycle_resid = cycle_part.reshape(8, 2, 4, 64).transpose(0, 2, 3, 1).reshape(32, 64, 2)
    move = [
        ((s * 4 + a) * 4 + hi * 2 + lo, (hi * 4 + lo * 2 + s) * 4 + a)
        for s in range(2)
        for a in range(4)
        for hi in range(2)
        for lo in range(2)
    ]
    ladder_resid = lax.ppermute(part, ("zl", "x", "zh"), move)
    return ladder_resid, cycle_resid


def solution(mesh):
    fine = Mesh(mesh.devices.reshape(8, 2, 4, 4, 2), ("y", "zl", "x", "zh", "core"))
    col, depth = ("zl", "x"), ("zh", "core")
    in_specs = (
        P("y", col, depth, None),
        P(depth, ("y", "zl", "x"), None),
        P(None, ("y", "zl", "x"), None),
        P(),
        P(),
        P(),
    )
    out_specs = (P(("y", "zl", "x", "zh", "core"), None), P(None, depth, ("y", "zl", "x")))
    return jax.shard_map(body, mesh=fine, in_specs=in_specs, out_specs=out_specs, check_vma=False)
```

```python
import jax
import jax.numpy as jnp
from jax import lax
from jax.experimental import pallas as pl
from jax.experimental.pallas import tpu as pltpu
from jax.sharding import Mesh, PartitionSpec as P

F32 = jnp.float32
BF16 = jnp.bfloat16
VMEM_LIMIT = 16 * 1024 * 1024
LADDER_LIMIT = 51 * 1024 * 1024


def split(v):
    hi = v.astype(BF16)
    lo = (v - hi.astype(F32)).astype(BF16)
    return hi, lo


def dot3(xh, xl, bh, bl):
    def mm(p, q):
        return jnp.dot(p, q, preferred_element_type=F32)

    return mm(xh, bh) + (mm(xh, bl) + mm(xl, bh))


def regroup_kernel(a_ref, o_ref):
    rows = a_ref.reshape(512, 128)
    lane = lax.broadcasted_iota(jnp.int32, (8, 128), 1)
    low = lane < 64
    even = (lane & 32) == 0

    def swap(keep, p, q, width):
        return (
            jnp.where(keep, p, pltpu.roll(q, width, 1)),
            jnp.where(keep, pltpu.roll(p, 128 - width, 1), q),
        )

    for q in range(16):
        v = [rows[pl.ds(4 * q + c, 8, stride=64), :] for c in range(4)]
        t0, t2 = swap(low, v[0], v[2], 64)
        t1, t3 = swap(low, v[1], v[3], 64)
        o0, o1 = swap(even, t0, t1, 32)
        o2, o3 = swap(even, t2, t3, 32)
        for g, o in enumerate((o0, o1, o2, o3)):
            o_ref[g, :, pl.ds(q * 128, 128)] = o


def regroup(amplitudes):
    a = amplitudes.reshape(4, 2, 2, 64, 512)
    return pl.pallas_call(
        regroup_kernel,
        grid=(4, 2),
        in_specs=[pl.BlockSpec((4, None, 2, 64, 128), lambda b, h: (0, h, 0, 0, b))],
        out_specs=pl.BlockSpec((4, None, 8, 2048), lambda b, h: (b, h, 0, 0)),
        out_shape=jax.ShapeDtypeStruct((16, 2, 8, 2048), F32),
        compiler_params=pltpu.CompilerParams(vmem_limit_bytes=VMEM_LIMIT),
        cost_estimate=pl.CostEstimate(flops=2**20, bytes_accessed=2**22, transcendentals=0),
    )(a)


def ladder_kernel(x_ref, b1, b1_far, b3, b3_far, b0, near, far, o_ref, held, sems):
    me = lax.axis_index("x")

    def copies(k):
        part = pl.ds(k * 16, 16)
        across = (near if k < 2 else far).at[pl.ds(k % 2 * 16, 16)]
        return (
            pltpu.make_async_copy(b0.at[part], held.at[me, part], sems.at[0, k]),
            pltpu.make_async_copy(across, held.at[lax.rem(me + 2, 4), part], sems.at[1, k]),
        )

    for k in range(4):
        for copy in copies(k):
            copy.start()
    for k in range(4):
        part, half = pl.ds(k * 16, 16), pl.ds(k % 2 * 16, 16)
        held[lax.rem(me + 1, 4), part] = (b3 if k < 2 else b3_far)[half]
        held[lax.rem(me + 3, 4), part] = (b1 if k < 2 else b1_far)[half]
        span = pl.ds(k * 512, 512)
        x = jnp.concatenate([x_ref[:, h, :, span].reshape(128, 512) for h in range(2)], axis=0)
        xh, xl = split(x)
        for copy in copies(k):
            copy.wait()
        b = [held[o, k * 16 + c] for c in range(16) for o in range(4)]
        bh, bl = split(jnp.concatenate(b, axis=0))
        total = dot3(xh, xl, bh, bl).reshape(2, 128, 640)
        if k == 0:
            o_ref[...] = total
        else:
            o_ref[...] += total


VMEM = pl.BlockSpec(memory_space=pltpu.VMEM)


def small(kernel, out_shape, *args, scratch=()):
    return pl.pallas_call(
        kernel,
        in_specs=[VMEM] * len(args),
        out_specs=VMEM if isinstance(out_shape, tuple) else [VMEM] * len(out_shape),
        out_shape=jax.ShapeDtypeStruct(out_shape, F32)
        if isinstance(out_shape, tuple)
        else [jax.ShapeDtypeStruct(shape, F32) for shape in out_shape],
        scratch_shapes=[pltpu.VMEM(shape, F32) for shape in scratch],
        compiler_params=pltpu.CompilerParams(vmem_limit_bytes=VMEM_LIMIT),
        cost_estimate=pl.CostEstimate(flops=2**18, bytes_accessed=2**20, transcendentals=0),
    )(*args)


def ladder(x, *blocks):
    anywhere = pl.BlockSpec(memory_space=pl.ANY)
    return pl.pallas_call(
        ladder_kernel,
        in_specs=[VMEM] * 5 + [anywhere] * 3,
        out_specs=VMEM,
        out_shape=jax.ShapeDtypeStruct((2, 128, 640), F32),
        scratch_shapes=[pltpu.VMEM((4, 64, 8, 640), F32), pltpu.SemaphoreType.DMA((2, 4))],
        compiler_params=pltpu.CompilerParams(vmem_limit_bytes=LADDER_LIMIT),
        cost_estimate=pl.CostEstimate(
            flops=3 * 2 * 256 * 2048 * 640, bytes_accessed=8 * 2**20, transcendentals=0
        ),
    )(x, *blocks)


def spread_kernel(w_ref, o_ref):
    core = lax.axis_index("core")
    for col in range(8):
        for y in range(8):
            o_ref[y * 8 + col] = w_ref[pl.ds(col * 4 + 2 * core, 2)]


def pack_kernel(part_ref, c0, c1, c2, c3, o_ref, ladder_sum, cycle_sum):
    ladder_sum[...] = part_ref[0] + part_ref[1]
    cycle_sum[...] = (c0[...] + c1[...]) + (c2[...] + c3[...])
    for d in range(64):
        o_ref[d, :, pl.ds(0, 640)] = ladder_sum[pl.ds(2 * d, 2), :]
        o_ref[d, :, pl.ds(640, 256)] = cycle_sum[pl.ds(d // 4 * 2, 2), :]


def finish_kernel(p_ref, ladder_ref, cycle_ref):
    zh = lax.axis_index("zh")
    total = [p_ref[d, :, pl.ds(0, 640)] for d in range(8)]
    for d in range(8, 64):
        total[d % 8] += p_ref[d, :, pl.ds(0, 640)]
    while len(total) > 1:
        total = [p + q for p, q in zip(total[::2], total[1::2])]
    ladder_ref[...] = total[0]
    for y in range(8):
        cycle_ref[y] = (
            p_ref[y * 8 + zh, :, pl.ds(640, 256)] + p_ref[y * 8 + 4 + zh, :, pl.ds(640, 256)]
        )


def cycle_kernel(occ_ref, a_ref, own_ref, other_ref, vir_ref, pair_ref, o_ref, turned):
    first = (lax.axis_index("zl") * 4 + lax.axis_index("x")) * 4
    core = lax.axis_index("core")
    total = jnp.zeros((256, 128), F32)
    for half, w_ref in ((core, own_ref), (1 - core, other_ref)):
        for s in range(2):
            k = 2 * half + s
            allowed = jnp.bitwise_xor(vir_ref[...], occ_ref[first + k]) == pair_ref[...]
            w = jnp.where(allowed, w_ref[:, s].reshape(512, 128), 0.0)
            ah, al = split(a_ref[:, k].reshape(256, 512))
            wh, wl = split(w)
            total = total + dot3(ah, al, wh, wl)
    turned[...] = total.T
    for x in range(4):
        to = lax.rem(x + 4 - lax.axis_index("x"), 4)
        for d in range(16):
            o_ref[to, pl.ds(2 * d, 2), :] = turned[pl.ds(8 * d + 2 * x, 2), :]


def cycle(occ, amplitudes, own, other, vir, pair):
    return pl.pallas_call(
        cycle_kernel,
        in_specs=[pl.BlockSpec(memory_space=pltpu.SMEM)] + [VMEM] * 5,
        out_specs=VMEM,
        out_shape=jax.ShapeDtypeStruct((4, 32, 256), F32),
        scratch_shapes=[pltpu.VMEM((128, 256), F32)],
        compiler_params=pltpu.CompilerParams(vmem_limit_bytes=VMEM_LIMIT),
        cost_estimate=pl.CostEstimate(
            flops=3 * 2 * 256 * 2048 * 128, bytes_accessed=3 * 2**20, transcendentals=0
        ),
    )(occ, amplitudes, own, other, vir, pair)


def exchange(v, axes):
    return lax.all_to_all(v, axes, split_axis=0, concat_axis=0, tiled=True)


def body(amplitudes, ladder_ints, cycle_ints, occ_irrep, vir_irrep, pair_irrep):
    own = exchange(small(spread_kernel, (64, 2, 8, 128), cycle_ints), ("y", "zl", "x"))

    ring = [[(i, (i + s) % 4) for i in range(4)] for s in range(4)]
    sent = regroup(amplitudes)
    _, ladder_ints = lax.optimization_barrier((sent, ladder_ints))
    sent, own = lax.optimization_barrier((sent, own))
    x = exchange(sent, ("y", "zl"))
    other = lax.ppermute(own, "core", [(0, 1), (1, 0)])
    lower, upper = ladder_ints[:32], ladder_ints[32:]
    b1 = lax.ppermute(lower, "x", ring[1])
    b3_far = lax.ppermute(upper, "x", ring[3])
    b1_far = lax.ppermute(upper, "x", ring[1])
    b3 = lax.ppermute(lower, "x", ring[3])
    near = lax.ppermute(b1, "x", ring[1])
    far = lax.ppermute(b3_far, "x", ring[3])

    vir = jnp.broadcast_to(vir_irrep[:, None], (512, 128))
    parts = cycle(occ_irrep, amplitudes, own, other, vir, pair_irrep[None])
    parts = [parts[0]] + [lax.ppermute(parts[s], "x", ring[s]) for s in (1, 2, 3)]

    part = ladder(x, b1, b1_far, b3, b3_far, ladder_ints, near, far)
    part = exchange(part, ("core",))
    both = small(pack_kernel, (64, 2, 896), part, *parts, scratch=[(128, 640), (32, 256)])
    both = exchange(both, ("y", "zl", "zh"))
    part, cycle_part = small(finish_kernel, [(2, 640), (8, 2, 256)], both)
    cycle_resid = cycle_part.reshape(8, 2, 4, 64).transpose(0, 2, 3, 1).reshape(32, 64, 2)
    move = [
        ((s * 4 + a) * 4 + hi * 2 + lo, (hi * 4 + lo * 2 + s) * 4 + a)
        for s in range(2)
        for a in range(4)
        for hi in range(2)
        for lo in range(2)
    ]
    ladder_resid = lax.ppermute(part, ("zl", "x", "zh"), move)
    return ladder_resid, cycle_resid


def solution(mesh):
    fine = Mesh(mesh.devices.reshape(8, 2, 4, 4, 2), ("y", "zl", "x", "zh", "core"))
    col, depth = ("zl", "x"), ("zh", "core")
    in_specs = (
        P("y", col, depth, None),
        P(depth, ("y", "zl", "x"), None),
        P(None, ("y", "zl", "x"), None),
        P(),
        P(),
        P(),
    )
    out_specs = (P(("y", "zl", "x", "zh", "core"), None), P(None, depth, ("y", "zl", "x")))
    return jax.shard_map(body, mesh=fine, in_specs=in_specs, out_specs=out_specs, check_vma=False)
```

```python
import jax
import jax.numpy as jnp
from jax import lax
from jax.experimental import pallas as pl
from jax.experimental.pallas import tpu as pltpu
from jax.sharding import Mesh, PartitionSpec as P

F32 = jnp.float32
BF16 = jnp.bfloat16
VMEM_LIMIT = 16 * 1024 * 1024
LADDER_LIMIT = 51 * 1024 * 1024


def split(v):
    hi = v.astype(BF16)
    lo = (v - hi.astype(F32)).astype(BF16)
    return hi, lo


def dot3(xh, xl, bh, bl):
    def mm(p, q):
        return jnp.dot(p, q, preferred_element_type=F32)

    return mm(xh, bh) + (mm(xh, bl) + mm(xl, bh))


def regroup_kernel(a_ref, o_ref):
    rows = a_ref.reshape(512, 128)
    lane = lax.broadcasted_iota(jnp.int32, (8, 128), 1)
    low = lane < 64
    even = (lane & 32) == 0

    def swap(keep, p, q, width):
        return (
            jnp.where(keep, p, pltpu.roll(q, width, 1)),
            jnp.where(keep, pltpu.roll(p, 128 - width, 1), q),
        )

    for q in range(16):
        v = [rows[pl.ds(4 * q + c, 8, stride=64), :] for c in range(4)]
        t0, t2 = swap(low, v[0], v[2], 64)
        t1, t3 = swap(low, v[1], v[3], 64)
        o0, o1 = swap(even, t0, t1, 32)
        o2, o3 = swap(even, t2, t3, 32)
        for g, o in enumerate((o0, o1, o2, o3)):
            o_ref[g, :, pl.ds(q * 128, 128)] = o


def regroup(amplitudes):
    a = amplitudes.reshape(4, 2, 2, 64, 512)
    return pl.pallas_call(
        regroup_kernel,
        grid=(4, 2),
        in_specs=[pl.BlockSpec((4, None, 2, 64, 128), lambda b, h: (0, h, 0, 0, b))],
        out_specs=pl.BlockSpec((4, None, 8, 2048), lambda b, h: (b, h, 0, 0)),
        out_shape=jax.ShapeDtypeStruct((16, 2, 8, 2048), F32),
        compiler_params=pltpu.CompilerParams(vmem_limit_bytes=VMEM_LIMIT),
        cost_estimate=pl.CostEstimate(flops=2**20, bytes_accessed=2**22, transcendentals=0),
    )(a)


def ladder_kernel(x_ref, b1, b1_far, b3, b3_far, near, far, b0, o_ref, held):
    me = lax.axis_index("x")
    for k in range(4):
        half = pl.ds(k % 2 * 16, 16)
        held[me] = b0[pl.ds(k * 16, 16)]
        held[lax.rem(me + 1, 4)] = (b3 if k < 2 else b3_far)[half]
        held[lax.rem(me + 2, 4)] = (near if k < 2 else far)[half]
        held[lax.rem(me + 3, 4)] = (b1 if k < 2 else b1_far)[half]
        span = pl.ds(k * 512, 512)
        x = jnp.concatenate([x_ref[:, h, :, span].reshape(128, 512) for h in range(2)], axis=0)
        xh, xl = split(x)
        b = [held[o, c] for c in range(16) for o in range(4)]
        bh, bl = split(jnp.concatenate(b, axis=0))
        total = dot3(xh, xl, bh, bl).reshape(2, 128, 640)
        if k == 0:
            o_ref[...] = total
        else:
            o_ref[...] += total


VMEM = pl.BlockSpec(memory_space=pltpu.VMEM)


def small(kernel, out_shape, *args, scratch=()):
    return pl.pallas_call(
        kernel,
        in_specs=[VMEM] * len(args),
        out_specs=VMEM if isinstance(out_shape, tuple) else [VMEM] * len(out_shape),
        out_shape=jax.ShapeDtypeStruct(out_shape, F32)
        if isinstance(out_shape, tuple)
        else [jax.ShapeDtypeStruct(shape, F32) for shape in out_shape],
        scratch_shapes=[pltpu.VMEM(shape, F32) for shape in scratch],
        compiler_params=pltpu.CompilerParams(vmem_limit_bytes=VMEM_LIMIT),
        cost_estimate=pl.CostEstimate(flops=2**18, bytes_accessed=2**20, transcendentals=0),
    )(*args)


def ladder(x, *blocks):
    return pl.pallas_call(
        ladder_kernel,
        in_specs=[VMEM] * 8,
        out_specs=VMEM,
        out_shape=jax.ShapeDtypeStruct((2, 128, 640), F32),
        scratch_shapes=[pltpu.VMEM((4, 16, 8, 640), F32)],
        compiler_params=pltpu.CompilerParams(vmem_limit_bytes=LADDER_LIMIT),
        cost_estimate=pl.CostEstimate(
            flops=3 * 2 * 256 * 2048 * 640, bytes_accessed=8 * 2**20, transcendentals=0
        ),
    )(x, *blocks)


def spread_kernel(w_ref, o_ref):
    core = lax.axis_index("core")
    for col in range(8):
        for y in range(8):
            o_ref[y * 8 + col] = w_ref[pl.ds(col * 4 + 2 * core, 2)]


def pack_kernel(part_ref, c0, c1, c2, c3, o_ref, ladder_sum, cycle_sum):
    ladder_sum[...] = part_ref[0] + part_ref[1]
    cycle_sum[...] = (c0[...] + c1[...]) + (c2[...] + c3[...])
    for d in range(64):
        o_ref[d, :, pl.ds(0, 640)] = ladder_sum[pl.ds(2 * d, 2), :]
        o_ref[d, :, pl.ds(640, 256)] = cycle_sum[pl.ds(d // 4 * 2, 2), :]


def finish_kernel(p_ref, ladder_ref, cycle_ref):
    zh = lax.axis_index("zh")
    total = [p_ref[d, :, pl.ds(0, 640)] for d in range(8)]
    for d in range(8, 64):
        total[d % 8] += p_ref[d, :, pl.ds(0, 640)]
    while len(total) > 1:
        total = [p + q for p, q in zip(total[::2], total[1::2])]
    ladder_ref[...] = total[0]
    for y in range(8):
        cycle_ref[y] = (
            p_ref[y * 8 + zh, :, pl.ds(640, 256)] + p_ref[y * 8 + 4 + zh, :, pl.ds(640, 256)]
        )


def cycle_kernel(occ_ref, a_ref, own_ref, other_ref, vir_ref, pair_ref, o_ref, turned):
    first = (lax.axis_index("zl") * 4 + lax.axis_index("x")) * 4
    core = lax.axis_index("core")
    total = jnp.zeros((256, 128), F32)
    for half, w_ref in ((core, own_ref), (1 - core, other_ref)):
        for s in range(2):
            k = 2 * half + s
            allowed = jnp.bitwise_xor(vir_ref[...], occ_ref[first + k]) == pair_ref[...]
            w = jnp.where(allowed, w_ref[:, s].reshape(512, 128), 0.0)
            ah, al = split(a_ref[:, k].reshape(256, 512))
            wh, wl = split(w)
            total = total + dot3(ah, al, wh, wl)
    turned[...] = total.T
    for x in range(4):
        to = lax.rem(x + 4 - lax.axis_index("x"), 4)
        for d in range(16):
            o_ref[to, pl.ds(2 * d, 2), :] = turned[pl.ds(8 * d + 2 * x, 2), :]


def cycle(occ, amplitudes, own, other, vir, pair):
    return pl.pallas_call(
        cycle_kernel,
        in_specs=[pl.BlockSpec(memory_space=pltpu.SMEM)] + [VMEM] * 5,
        out_specs=VMEM,
        out_shape=jax.ShapeDtypeStruct((4, 32, 256), F32),
        scratch_shapes=[pltpu.VMEM((128, 256), F32)],
        compiler_params=pltpu.CompilerParams(vmem_limit_bytes=VMEM_LIMIT),
        cost_estimate=pl.CostEstimate(
            flops=3 * 2 * 256 * 2048 * 128, bytes_accessed=3 * 2**20, transcendentals=0
        ),
    )(occ, amplitudes, own, other, vir, pair)


def exchange(v, axes):
    return lax.all_to_all(v, axes, split_axis=0, concat_axis=0, tiled=True)


def body(amplitudes, ladder_ints, cycle_ints, occ_irrep, vir_irrep, pair_irrep):
    own = exchange(small(spread_kernel, (64, 2, 8, 128), cycle_ints), ("y", "zl", "x"))

    ring = [[(i, (i + s) % 4) for i in range(4)] for s in range(4)]
    sent = regroup(amplitudes)
    _, ladder_ints = lax.optimization_barrier((sent, ladder_ints))
    sent, own = lax.optimization_barrier((sent, own))
    x = exchange(sent, ("y", "zl"))
    other = lax.ppermute(own, "core", [(0, 1), (1, 0)])
    lower, upper = ladder_ints[:32], ladder_ints[32:]
    b1 = lax.ppermute(lower, "x", ring[1])
    b3_far = lax.ppermute(upper, "x", ring[3])
    b1_far = lax.ppermute(upper, "x", ring[1])
    b3 = lax.ppermute(lower, "x", ring[3])
    near = lax.ppermute(b1, "x", ring[1])
    far = lax.ppermute(b3_far, "x", ring[3])

    vir = jnp.broadcast_to(vir_irrep[:, None], (512, 128))
    parts = cycle(occ_irrep, amplitudes, own, other, vir, pair_irrep[None])
    parts = [parts[0]] + [lax.ppermute(parts[s], "x", ring[s]) for s in (1, 2, 3)]

    part = ladder(x, b1, b1_far, b3, b3_far, near, far, ladder_ints)
    part = exchange(part, ("core",))
    both = small(pack_kernel, (64, 2, 896), part, *parts, scratch=[(128, 640), (32, 256)])
    both = exchange(both, ("y", "zl", "zh"))
    part, cycle_part = small(finish_kernel, [(2, 640), (8, 2, 256)], both)
    cycle_resid = cycle_part.reshape(8, 2, 4, 64).transpose(0, 2, 3, 1).reshape(32, 64, 2)
    move = [
        ((s * 4 + a) * 4 + hi * 2 + lo, (hi * 4 + lo * 2 + s) * 4 + a)
        for s in range(2)
        for a in range(4)
        for hi in range(2)
        for lo in range(2)
    ]
    ladder_resid = lax.ppermute(part, ("zl", "x", "zh"), move)
    return ladder_resid, cycle_resid


def solution(mesh):
    fine = Mesh(mesh.devices.reshape(8, 2, 4, 4, 2), ("y", "zl", "x", "zh", "core"))
    col, depth = ("zl", "x"), ("zh", "core")
    in_specs = (
        P("y", col, depth, None),
        P(depth, ("y", "zl", "x"), None),
        P(None, ("y", "zl", "x"), None),
        P(),
        P(),
        P(),
    )
    out_specs = (P(("y", "zl", "x", "zh", "core"), None), P(None, depth, ("y", "zl", "x")))
    return jax.shard_map(body, mesh=fine, in_specs=in_specs, out_specs=out_specs, check_vma=False)
```

```python
import jax
import jax.numpy as jnp
from jax import lax
from jax.experimental import pallas as pl
from jax.experimental.pallas import tpu as pltpu
from jax.sharding import Mesh, PartitionSpec as P

F32 = jnp.float32
BF16 = jnp.bfloat16
VMEM_LIMIT = 16 * 1024 * 1024
LADDER_LIMIT = 51 * 1024 * 1024
SPREAD_LIMIT = 60 * 1024 * 1024


def split(v):
    hi = v.astype(BF16)
    lo = (v - hi.astype(F32)).astype(BF16)
    return hi, lo


def dot3(xh, xl, bh, bl):
    def mm(p, q):
        return jnp.dot(p, q, preferred_element_type=F32)

    return mm(xh, bh) + (mm(xh, bl) + mm(xl, bh))


def regroup_kernel(a_ref, o_ref):
    rows = a_ref.reshape(512, 128)
    lane = lax.broadcasted_iota(jnp.int32, (8, 128), 1)
    low = lane < 64
    even = (lane & 32) == 0

    def swap(keep, p, q, width):
        return (
            jnp.where(keep, p, pltpu.roll(q, width, 1)),
            jnp.where(keep, pltpu.roll(p, 128 - width, 1), q),
        )

    for q in range(16):
        v = [rows[pl.ds(4 * q + c, 8, stride=64), :] for c in range(4)]
        t0, t2 = swap(low, v[0], v[2], 64)
        t1, t3 = swap(low, v[1], v[3], 64)
        o0, o1 = swap(even, t0, t1, 32)
        o2, o3 = swap(even, t2, t3, 32)
        for g, o in enumerate((o0, o1, o2, o3)):
            o_ref[g, :, pl.ds(q * 128, 128)] = o


def regroup(amplitudes):
    a = amplitudes.reshape(4, 2, 2, 64, 512)
    return pl.pallas_call(
        regroup_kernel,
        grid=(4, 2),
        in_specs=[pl.BlockSpec((4, None, 2, 64, 128), lambda b, h: (0, h, 0, 0, b))],
        out_specs=pl.BlockSpec((4, None, 8, 2048), lambda b, h: (b, h, 0, 0)),
        out_shape=jax.ShapeDtypeStruct((16, 2, 8, 2048), F32),
        compiler_params=pltpu.CompilerParams(vmem_limit_bytes=VMEM_LIMIT),
        cost_estimate=pl.CostEstimate(flops=2**20, bytes_accessed=2**22, transcendentals=0),
    )(a)


def ladder_kernel(x_ref, b1, b1_far, b3, near, b0, b3_far, far, o_ref, held, sems):
    me = lax.axis_index("x")

    def copies(k):
        part, half = pl.ds(k * 16, 16), pl.ds(k % 2 * 16, 16)
        found = [(0, b0.at[part])]
        if k >= 2:
            found += [(1, b3_far.at[half]), (2, far.at[half])]
        return [
            pltpu.make_async_copy(b, held.at[lax.rem(me + s, 4), part], sems.at[s, k])
            for s, b in found
        ]

    for k in range(4):
        for copy in copies(k):
            copy.start()
    for k in range(4):
        part, half = pl.ds(k * 16, 16), pl.ds(k % 2 * 16, 16)
        held[lax.rem(me + 3, 4), part] = (b1 if k < 2 else b1_far)[half]
        if k < 2:
            held[lax.rem(me + 1, 4), part] = b3[half]
            held[lax.rem(me + 2, 4), part] = near[half]
        span = pl.ds(k * 512, 512)
        x = jnp.concatenate([x_ref[:, h, :, span].reshape(128, 512) for h in range(2)], axis=0)
        xh, xl = split(x)
        for copy in copies(k):
            copy.wait()
        b = [held[o, k * 16 + c] for c in range(16) for o in range(4)]
        bh, bl = split(jnp.concatenate(b, axis=0))
        total = dot3(xh, xl, bh, bl).reshape(2, 128, 640)
        if k == 0:
            o_ref[...] = total
        else:
            o_ref[...] += total


VMEM = pl.BlockSpec(memory_space=pltpu.VMEM)


def small(kernel, out_shape, *args, scratch=()):
    return pl.pallas_call(
        kernel,
        in_specs=[VMEM] * len(args),
        out_specs=VMEM if isinstance(out_shape, tuple) else [VMEM] * len(out_shape),
        out_shape=jax.ShapeDtypeStruct(out_shape, F32)
        if isinstance(out_shape, tuple)
        else [jax.ShapeDtypeStruct(shape, F32) for shape in out_shape],
        scratch_shapes=[pltpu.VMEM(shape, F32) for shape in scratch],
        compiler_params=pltpu.CompilerParams(vmem_limit_bytes=VMEM_LIMIT),
        cost_estimate=pl.CostEstimate(flops=2**18, bytes_accessed=2**20, transcendentals=0),
    )(*args)


def ladder(x, *blocks):
    anywhere = pl.BlockSpec(memory_space=pl.ANY)
    return pl.pallas_call(
        ladder_kernel,
        in_specs=[VMEM] * 5 + [anywhere] * 3,
        out_specs=VMEM,
        out_shape=jax.ShapeDtypeStruct((2, 128, 640), F32),
        scratch_shapes=[pltpu.VMEM((4, 64, 8, 640), F32), pltpu.SemaphoreType.DMA((3, 4))],
        compiler_params=pltpu.CompilerParams(vmem_limit_bytes=LADDER_LIMIT),
        cost_estimate=pl.CostEstimate(
            flops=3 * 2 * 256 * 2048 * 640, bytes_accessed=8 * 2**20, transcendentals=0
        ),
    )(x, *blocks)


def spread_kernel(w_hbm, o_ref, held, sem):
    copy = pltpu.make_async_copy(w_hbm.at[:, pl.ds(2 * lax.axis_index("core"), 2)], held, sem)
    copy.start()
    copy.wait()
    for y in range(8):
        o_ref[pl.ds(y * 8, 8)] = held[...]


def spread(w):
    return pl.pallas_call(
        spread_kernel,
        in_specs=[pl.BlockSpec(memory_space=pl.ANY)],
        out_specs=VMEM,
        out_shape=jax.ShapeDtypeStruct((64, 2, 8, 128), F32),
        scratch_shapes=[pltpu.VMEM((8, 2, 8, 128), F32), pltpu.SemaphoreType.DMA],
        compiler_params=pltpu.CompilerParams(vmem_limit_bytes=SPREAD_LIMIT),
        cost_estimate=pl.CostEstimate(flops=0, bytes_accessed=2**20, transcendentals=0),
    )(w.reshape(8, 4, 8, 128))


def pack_kernel(part_ref, c0, c1, c2, c3, o_ref, ladder_sum, cycle_sum):
    ladder_sum[...] = part_ref[0] + part_ref[1]
    cycle_sum[...] = (c0[...] + c1[...]) + (c2[...] + c3[...])
    for d in range(64):
        o_ref[d, :, pl.ds(0, 640)] = ladder_sum[pl.ds(2 * d, 2), :]
        o_ref[d, :, pl.ds(640, 256)] = cycle_sum[pl.ds(d // 4 * 2, 2), :]


def finish_kernel(p_ref, ladder_ref, cycle_ref):
    zh = lax.axis_index("zh")
    total = [p_ref[d, :, pl.ds(0, 640)] for d in range(8)]
    for d in range(8, 64):
        total[d % 8] += p_ref[d, :, pl.ds(0, 640)]
    while len(total) > 1:
        total = [p + q for p, q in zip(total[::2], total[1::2])]
    ladder_ref[...] = total[0]
    for y in range(8):
        cycle_ref[y] = (
            p_ref[y * 8 + zh, :, pl.ds(640, 256)] + p_ref[y * 8 + 4 + zh, :, pl.ds(640, 256)]
        )


def cycle_kernel(occ_ref, a_ref, own_ref, other_ref, vir_ref, pair_ref, o_ref, turned):
    first = (lax.axis_index("zl") * 4 + lax.axis_index("x")) * 4
    core = lax.axis_index("core")
    total = jnp.zeros((256, 128), F32)
    for half, w_ref in ((core, own_ref), (1 - core, other_ref)):
        for s in range(2):
            k = 2 * half + s
            allowed = jnp.bitwise_xor(vir_ref[...], occ_ref[first + k]) == pair_ref[...]
            w = jnp.where(allowed, w_ref[:, s].reshape(512, 128), 0.0)
            ah, al = split(a_ref[:, k].reshape(256, 512))
            wh, wl = split(w)
            total = total + dot3(ah, al, wh, wl)
    turned[...] = total.T
    for x in range(4):
        to = lax.rem(x + 4 - lax.axis_index("x"), 4)
        for d in range(16):
            o_ref[to, pl.ds(2 * d, 2), :] = turned[pl.ds(8 * d + 2 * x, 2), :]


def cycle(occ, amplitudes, own, other, vir, pair):
    return pl.pallas_call(
        cycle_kernel,
        in_specs=[pl.BlockSpec(memory_space=pltpu.SMEM)] + [VMEM] * 5,
        out_specs=VMEM,
        out_shape=jax.ShapeDtypeStruct((4, 32, 256), F32),
        scratch_shapes=[pltpu.VMEM((128, 256), F32)],
        compiler_params=pltpu.CompilerParams(vmem_limit_bytes=VMEM_LIMIT),
        cost_estimate=pl.CostEstimate(
            flops=3 * 2 * 256 * 2048 * 128, bytes_accessed=3 * 2**20, transcendentals=0
        ),
    )(occ, amplitudes, own, other, vir, pair)


def exchange(v, axes):
    return lax.all_to_all(v, axes, split_axis=0, concat_axis=0, tiled=True)


def body(amplitudes, ladder_ints, cycle_ints, occ_irrep, vir_irrep, pair_irrep):
    own = exchange(spread(cycle_ints), ("y", "zl", "x"))

    ring = [[(i, (i + s) % 4) for i in range(4)] for s in range(4)]
    sent = regroup(amplitudes)
    _, ladder_ints = lax.optimization_barrier((sent, ladder_ints))
    sent, own = lax.optimization_barrier((sent, own))
    x = exchange(sent, ("y", "zl"))
    other = lax.ppermute(own, "core", [(0, 1), (1, 0)])
    lower, upper = ladder_ints[:32], ladder_ints[32:]
    b1 = lax.ppermute(lower, "x", ring[1])
    b3_far = lax.ppermute(upper, "x", ring[3])
    b1_far = lax.ppermute(upper, "x", ring[1])
    b3 = lax.ppermute(lower, "x", ring[3])
    near = lax.ppermute(b1, "x", ring[1])
    far = lax.ppermute(b3_far, "x", ring[3])

    vir = jnp.broadcast_to(vir_irrep[:, None], (512, 128))
    parts = cycle(occ_irrep, amplitudes, own, other, vir, pair_irrep[None])
    parts = [parts[0]] + [lax.ppermute(parts[s], "x", ring[s]) for s in (1, 2, 3)]

    part = ladder(x, b1, b1_far, b3, near, ladder_ints, b3_far, far)
    part = exchange(part, ("core",))
    both = small(pack_kernel, (64, 2, 896), part, *parts, scratch=[(128, 640), (32, 256)])
    both = exchange(both, ("y", "zl", "zh"))
    part, cycle_part = small(finish_kernel, [(2, 640), (8, 2, 256)], both)
    cycle_resid = cycle_part.reshape(8, 2, 4, 64).transpose(0, 2, 3, 1).reshape(32, 64, 2)
    move = [
        ((s * 4 + a) * 4 + hi * 2 + lo, (hi * 4 + lo * 2 + s) * 4 + a)
        for s in range(2)
        for a in range(4)
        for hi in range(2)
        for lo in range(2)
    ]
    ladder_resid = lax.ppermute(part, ("zl", "x", "zh"), move)
    return ladder_resid, cycle_resid


def solution(mesh):
    fine = Mesh(mesh.devices.reshape(8, 2, 4, 4, 2), ("y", "zl", "x", "zh", "core"))
    col, depth = ("zl", "x"), ("zh", "core")
    in_specs = (
        P("y", col, depth, None),
        P(depth, ("y", "zl", "x"), None),
        P(None, ("y", "zl", "x"), None),
        P(),
        P(),
        P(),
    )
    out_specs = (P(("y", "zl", "x", "zh", "core"), None), P(None, depth, ("y", "zl", "x")))
    return jax.shard_map(body, mesh=fine, in_specs=in_specs, out_specs=out_specs, check_vma=False)
```

```python
import jax
import jax.numpy as jnp
from jax import lax
from jax.experimental import pallas as pl
from jax.experimental.pallas import tpu as pltpu
from jax.sharding import Mesh, PartitionSpec as P

F32 = jnp.float32
BF16 = jnp.bfloat16
VMEM_LIMIT = 16 * 1024 * 1024
LADDER_LIMIT = 51 * 1024 * 1024
SPREAD_LIMIT = 60 * 1024 * 1024


def split(v):
    hi = v.astype(BF16)
    lo = (v - hi.astype(F32)).astype(BF16)
    return hi, lo


def dot3(xh, xl, bh, bl):
    def mm(p, q):
        return jnp.dot(p, q, preferred_element_type=F32)

    return mm(xh, bh) + (mm(xh, bl) + mm(xl, bh))


def regroup_kernel(a_ref, o_ref):
    rows = a_ref.reshape(512, 128)
    lane = lax.broadcasted_iota(jnp.int32, (8, 128), 1)
    low = lane < 64
    even = (lane & 32) == 0

    def swap(keep, p, q, width):
        return (
            jnp.where(keep, p, pltpu.roll(q, width, 1)),
            jnp.where(keep, pltpu.roll(p, 128 - width, 1), q),
        )

    for q in range(16):
        v = [rows[pl.ds(4 * q + c, 8, stride=64), :] for c in range(4)]
        t0, t2 = swap(low, v[0], v[2], 64)
        t1, t3 = swap(low, v[1], v[3], 64)
        o0, o1 = swap(even, t0, t1, 32)
        o2, o3 = swap(even, t2, t3, 32)
        for g, o in enumerate((o0, o1, o2, o3)):
            o_ref[g, :, pl.ds(q * 128, 128)] = o


def regroup(amplitudes):
    a = amplitudes.reshape(4, 2, 2, 64, 512)
    return pl.pallas_call(
        regroup_kernel,
        grid=(4, 2),
        in_specs=[pl.BlockSpec((4, None, 2, 64, 128), lambda b, h: (0, h, 0, 0, b))],
        out_specs=pl.BlockSpec((4, None, 8, 2048), lambda b, h: (b, h, 0, 0)),
        out_shape=jax.ShapeDtypeStruct((16, 2, 8, 2048), F32),
        compiler_params=pltpu.CompilerParams(vmem_limit_bytes=VMEM_LIMIT),
        cost_estimate=pl.CostEstimate(flops=2**20, bytes_accessed=2**22, transcendentals=0),
    )(a)


def ladder_kernel(x_ref, b1, b1_far, b3, near, b0, b3_far, far, o_ref, held, sems):
    me = lax.axis_index("x")

    def copies(k):
        part, half = pl.ds(k * 16, 16), pl.ds(k % 2 * 16, 16)
        found = [(0, b0.at[part])]
        if k >= 2:
            found += [(1, b3_far.at[half]), (2, far.at[half])]
        return [
            pltpu.make_async_copy(b, held.at[lax.rem(me + s, 4), part], sems.at[s, k])
            for s, b in found
        ]

    for k in range(4):
        for copy in copies(k):
            copy.start()
    for k in range(4):
        part, half = pl.ds(k * 16, 16), pl.ds(k % 2 * 16, 16)
        held[lax.rem(me + 3, 4), part] = (b1 if k < 2 else b1_far)[half]
        if k < 2:
            held[lax.rem(me + 1, 4), part] = b3[half]
            held[lax.rem(me + 2, 4), part] = near[half]
        span = pl.ds(k * 512, 512)
        x = jnp.concatenate([x_ref[:, h, :, span].reshape(128, 512) for h in range(2)], axis=0)
        xh, xl = split(x)
        for copy in copies(k):
            copy.wait()
        b = [held[o, k * 16 + c] for c in range(16) for o in range(4)]
        bh, bl = split(jnp.concatenate(b, axis=0))
        total = dot3(xh, xl, bh, bl).reshape(2, 128, 640)
        if k == 0:
            o_ref[...] = total
        else:
            o_ref[...] += total


VMEM = pl.BlockSpec(memory_space=pltpu.VMEM)


def small(kernel, out_shape, *args, scratch=()):
    return pl.pallas_call(
        kernel,
        in_specs=[VMEM] * len(args),
        out_specs=VMEM if isinstance(out_shape, tuple) else [VMEM] * len(out_shape),
        out_shape=jax.ShapeDtypeStruct(out_shape, F32)
        if isinstance(out_shape, tuple)
        else [jax.ShapeDtypeStruct(shape, F32) for shape in out_shape],
        scratch_shapes=[pltpu.VMEM(shape, F32) for shape in scratch],
        compiler_params=pltpu.CompilerParams(vmem_limit_bytes=VMEM_LIMIT),
        cost_estimate=pl.CostEstimate(flops=2**18, bytes_accessed=2**20, transcendentals=0),
    )(*args)


def ladder(x, *blocks):
    anywhere = pl.BlockSpec(memory_space=pl.ANY)
    return pl.pallas_call(
        ladder_kernel,
        in_specs=[VMEM] * 5 + [anywhere] * 3,
        out_specs=VMEM,
        out_shape=jax.ShapeDtypeStruct((2, 128, 640), F32),
        scratch_shapes=[pltpu.VMEM((4, 64, 8, 640), F32), pltpu.SemaphoreType.DMA((3, 4))],
        compiler_params=pltpu.CompilerParams(vmem_limit_bytes=LADDER_LIMIT),
        cost_estimate=pl.CostEstimate(
            flops=3 * 2 * 256 * 2048 * 640, bytes_accessed=8 * 2**20, transcendentals=0
        ),
    )(x, *blocks)


def spread_kernel(w_hbm, o_ref, held, sem):
    copy = pltpu.make_async_copy(w_hbm.at[:, pl.ds(2 * lax.axis_index("core"), 2)], held, sem)
    copy.start()
    copy.wait()
    for y in range(8):
        o_ref[pl.ds(y * 8, 8)] = held[...]


def spread(w):
    return pl.pallas_call(
        spread_kernel,
        in_specs=[pl.BlockSpec(memory_space=pl.ANY)],
        out_specs=VMEM,
        out_shape=jax.ShapeDtypeStruct((64, 2, 8, 128), F32),
        scratch_shapes=[pltpu.VMEM((8, 2, 8, 128), F32), pltpu.SemaphoreType.DMA],
        compiler_params=pltpu.CompilerParams(vmem_limit_bytes=SPREAD_LIMIT),
        cost_estimate=pl.CostEstimate(flops=0, bytes_accessed=2**20, transcendentals=0),
    )(w.reshape(8, 4, 8, 128))


def cores_kernel(p_ref, o_ref, total):
    total[...] = p_ref[0] + p_ref[1]
    for y in range(8):
        for d in range(8):
            o_ref[d, y] = total[pl.ds(16 * y + 2 * d, 2), :]


def depth_kernel(p_ref, o_ref):
    for y in range(8):
        p = [p_ref[s, y] for s in range(8)]
        o_ref[y] = ((p[0] + p[1]) + (p[2] + p[3])) + ((p[4] + p[5]) + (p[6] + p[7]))


def fold_kernel(c0, c1, c2, c3, keep_ref, give_ref):
    zl = lax.axis_index("zl")
    keep_ref[...] = (c0[zl] + c1[zl]) + (c2[zl] + c3[zl])
    give_ref[...] = (c0[1 - zl] + c1[1 - zl]) + (c2[1 - zl] + c3[1 - zl])


def pack_kernel(l_ref, keep_ref, got_ref, o_ref):
    for y in range(8):
        rows = pl.ds(2 * y, 2)
        o_ref[y, :, pl.ds(0, 640)] = l_ref[y]
        o_ref[y, :, pl.ds(640, 256)] = keep_ref[rows, :] + got_ref[rows, :]


def finish_kernel(p_ref, ladder_ref, cycle_ref):
    p = [p_ref[y, :, pl.ds(0, 640)] for y in range(8)]
    ladder_ref[...] = ((p[0] + p[1]) + (p[2] + p[3])) + ((p[4] + p[5]) + (p[6] + p[7]))
    cycle_ref[...] = p_ref[:, :, pl.ds(640, 256)]


def cycle_kernel(occ_ref, a_ref, own_ref, other_ref, vir_ref, pair_ref, o_ref, turned):
    first = (lax.axis_index("zl") * 4 + lax.axis_index("x")) * 4
    core = lax.axis_index("core")
    total = jnp.zeros((256, 128), F32)
    for half, w_ref in ((core, own_ref), (1 - core, other_ref)):
        for s in range(2):
            k = 2 * half + s
            allowed = jnp.bitwise_xor(vir_ref[...], occ_ref[first + k]) == pair_ref[...]
            w = jnp.where(allowed, w_ref[:, s].reshape(512, 128), 0.0)
            ah, al = split(a_ref[:, k].reshape(256, 512))
            wh, wl = split(w)
            total = total + dot3(ah, al, wh, wl)
    turned[...] = total.T
    for x in range(4):
        to = lax.rem(x + 4 - lax.axis_index("x"), 4)
        for zl in range(2):
            for y in range(8):
                rows = turned[pl.ds(16 * y + 8 * zl + 2 * x, 2), :]
                o_ref[to, zl, pl.ds(2 * y, 2), :] = rows


def cycle(occ, amplitudes, own, other, vir, pair):
    return pl.pallas_call(
        cycle_kernel,
        in_specs=[pl.BlockSpec(memory_space=pltpu.SMEM)] + [VMEM] * 5,
        out_specs=VMEM,
        out_shape=jax.ShapeDtypeStruct((4, 2, 16, 256), F32),
        scratch_shapes=[pltpu.VMEM((128, 256), F32)],
        compiler_params=pltpu.CompilerParams(vmem_limit_bytes=VMEM_LIMIT),
        cost_estimate=pl.CostEstimate(
            flops=3 * 2 * 256 * 2048 * 128, bytes_accessed=3 * 2**20, transcendentals=0
        ),
    )(occ, amplitudes, own, other, vir, pair)


def exchange(v, axes):
    return lax.all_to_all(v, axes, split_axis=0, concat_axis=0, tiled=True)


def body(amplitudes, ladder_ints, cycle_ints, occ_irrep, vir_irrep, pair_irrep):
    own = exchange(spread(cycle_ints), ("y", "zl", "x"))

    ring = [[(i, (i + s) % 4) for i in range(4)] for s in range(4)]
    sent = regroup(amplitudes)
    _, ladder_ints = lax.optimization_barrier((sent, ladder_ints))
    sent, own = lax.optimization_barrier((sent, own))
    x = exchange(sent, ("y", "zl"))
    other = lax.ppermute(own, "core", [(0, 1), (1, 0)])
    lower, upper = ladder_ints[:32], ladder_ints[32:]
    b1 = lax.ppermute(lower, "x", ring[1])
    b3_far = lax.ppermute(upper, "x", ring[3])
    b1_far = lax.ppermute(upper, "x", ring[1])
    b3 = lax.ppermute(lower, "x", ring[3])
    near = lax.ppermute(b1, "x", ring[1])
    far = lax.ppermute(b3_far, "x", ring[3])

    vir = jnp.broadcast_to(vir_irrep[:, None], (512, 128))
    parts = cycle(occ_irrep, amplitudes, own, other, vir, pair_irrep[None])
    parts = [parts[0]] + [lax.ppermute(parts[s], "x", ring[s]) for s in (1, 2, 3)]

    part = ladder(x, b1, b1_far, b3, near, ladder_ints, b3_far, far)
    _, *parts = lax.optimization_barrier((part, *parts))
    keep, give = small(fold_kernel, [(16, 256), (16, 256)], *parts)
    got = lax.ppermute(give, "zl", [(0, 1), (1, 0)])
    part, keep = lax.optimization_barrier((exchange(part, ("core",)), keep))
    part = small(cores_kernel, (8, 8, 2, 640), part, scratch=[(128, 640)])
    part, got = lax.optimization_barrier((exchange(part, ("zl", "zh")), got))
    part = small(depth_kernel, (8, 2, 640), part)
    move = [
        ((s * 4 + a) * 4 + hi * 2 + lo, (hi * 4 + lo * 2 + s) * 4 + a)
        for s in range(2)
        for a in range(4)
        for hi in range(2)
        for lo in range(2)
    ]
    part = lax.ppermute(part, ("zl", "x", "zh"), move)
    both = exchange(small(pack_kernel, (8, 2, 896), part, keep, got), ("y",))
    ladder_resid, cycle_part = small(finish_kernel, [(2, 640), (8, 2, 256)], both)
    cycle_resid = cycle_part.reshape(8, 2, 4, 64).transpose(0, 2, 3, 1).reshape(32, 64, 2)
    return ladder_resid, cycle_resid


def solution(mesh):
    fine = Mesh(mesh.devices.reshape(8, 2, 4, 4, 2), ("y", "zl", "x", "zh", "core"))
    col, depth = ("zl", "x"), ("zh", "core")
    in_specs = (
        P("y", col, depth, None),
        P(depth, ("y", "zl", "x"), None),
        P(None, ("y", "zl", "x"), None),
        P(),
        P(),
        P(),
    )
    out_specs = (P(("y", "zl", "x", "zh", "core"), None), P(None, depth, ("y", "zl", "x")))
    return jax.shard_map(body, mesh=fine, in_specs=in_specs, out_specs=out_specs, check_vma=False)
```

```python
import jax
import jax.numpy as jnp
from jax import lax
from jax.experimental import pallas as pl
from jax.experimental.pallas import tpu as pltpu
from jax.sharding import Mesh, PartitionSpec as P

F32 = jnp.float32
BF16 = jnp.bfloat16
VMEM_LIMIT = 16 * 1024 * 1024
LADDER_LIMIT = 51 * 1024 * 1024
SPREAD_LIMIT = 60 * 1024 * 1024


def split(v):
    hi = v.astype(BF16)
    lo = (v - hi.astype(F32)).astype(BF16)
    return hi, lo


def dot3(xh, xl, bh, bl):
    def mm(p, q):
        return jnp.dot(p, q, preferred_element_type=F32)

    return mm(xh, bh) + (mm(xh, bl) + mm(xl, bh))


def regroup_kernel(a_ref, o_ref):
    rows = a_ref.reshape(512, 128)
    lane = lax.broadcasted_iota(jnp.int32, (8, 128), 1)
    low = lane < 64
    even = (lane & 32) == 0

    def swap(keep, p, q, width):
        return (
            jnp.where(keep, p, pltpu.roll(q, width, 1)),
            jnp.where(keep, pltpu.roll(p, 128 - width, 1), q),
        )

    for q in range(16):
        v = [rows[pl.ds(4 * q + c, 8, stride=64), :] for c in range(4)]
        t0, t2 = swap(low, v[0], v[2], 64)
        t1, t3 = swap(low, v[1], v[3], 64)
        o0, o1 = swap(even, t0, t1, 32)
        o2, o3 = swap(even, t2, t3, 32)
        for g, o in enumerate((o0, o1, o2, o3)):
            o_ref[g, :, pl.ds(q * 128, 128)] = o


def regroup(amplitudes):
    a = amplitudes.reshape(4, 2, 2, 64, 512)
    return pl.pallas_call(
        regroup_kernel,
        grid=(4, 2),
        in_specs=[pl.BlockSpec((4, None, 2, 64, 128), lambda b, h: (0, h, 0, 0, b))],
        out_specs=pl.BlockSpec((4, None, 8, 2048), lambda b, h: (b, h, 0, 0)),
        out_shape=jax.ShapeDtypeStruct((16, 2, 8, 2048), F32),
        compiler_params=pltpu.CompilerParams(vmem_limit_bytes=VMEM_LIMIT),
        cost_estimate=pl.CostEstimate(flops=2**20, bytes_accessed=2**22, transcendentals=0),
    )(a)


def ladder_kernel(b1, b1_far, b3, near, x_hbm, b0, b3_far, far, o_ref, x_ref, held, sems):
    me = lax.axis_index("x")

    def copies(k):
        part, half = pl.ds(k * 16, 16), pl.ds(k % 2 * 16, 16)
        span = pl.ds(k * 512, 512)
        found = [(0, b0.at[part])]
        if k >= 2:
            found += [(1, b3_far.at[half]), (2, far.at[half])]
        return [
            pltpu.make_async_copy(x_hbm.at[:, :, :, span], x_ref.at[:, :, :, span], sems.at[3, k])
        ] + [
            pltpu.make_async_copy(b, held.at[lax.rem(me + s, 4), part], sems.at[s, k])
            for s, b in found
        ]

    for k in range(4):
        for copy in copies(k):
            copy.start()
    for k in range(4):
        part, half = pl.ds(k * 16, 16), pl.ds(k % 2 * 16, 16)
        held[lax.rem(me + 3, 4), part] = (b1 if k < 2 else b1_far)[half]
        if k < 2:
            held[lax.rem(me + 1, 4), part] = b3[half]
            held[lax.rem(me + 2, 4), part] = near[half]
        span = pl.ds(k * 512, 512)
        for copy in copies(k):
            copy.wait()
        x = jnp.concatenate([x_ref[:, h, :, span].reshape(128, 512) for h in range(2)], axis=0)
        xh, xl = split(x)
        b = [held[o, k * 16 + c] for c in range(16) for o in range(4)]
        bh, bl = split(jnp.concatenate(b, axis=0))
        total = dot3(xh, xl, bh, bl).reshape(2, 128, 640)
        if k == 0:
            o_ref[...] = total
        else:
            o_ref[...] += total


VMEM = pl.BlockSpec(memory_space=pltpu.VMEM)


def small(kernel, out_shape, *args, scratch=()):
    return pl.pallas_call(
        kernel,
        in_specs=[VMEM] * len(args),
        out_specs=VMEM if isinstance(out_shape, tuple) else [VMEM] * len(out_shape),
        out_shape=jax.ShapeDtypeStruct(out_shape, F32)
        if isinstance(out_shape, tuple)
        else [jax.ShapeDtypeStruct(shape, F32) for shape in out_shape],
        scratch_shapes=[pltpu.VMEM(shape, F32) for shape in scratch],
        compiler_params=pltpu.CompilerParams(vmem_limit_bytes=VMEM_LIMIT),
        cost_estimate=pl.CostEstimate(flops=2**18, bytes_accessed=2**20, transcendentals=0),
    )(*args)


def ladder(*blocks):
    anywhere = pl.BlockSpec(memory_space=pl.ANY)
    return pl.pallas_call(
        ladder_kernel,
        in_specs=[VMEM] * 4 + [anywhere] * 4,
        out_specs=VMEM,
        out_shape=jax.ShapeDtypeStruct((2, 128, 640), F32),
        scratch_shapes=[
            pltpu.VMEM((16, 2, 8, 2048), F32),
            pltpu.VMEM((4, 64, 8, 640), F32),
            pltpu.SemaphoreType.DMA((4, 4)),
        ],
        compiler_params=pltpu.CompilerParams(vmem_limit_bytes=LADDER_LIMIT),
        cost_estimate=pl.CostEstimate(
            flops=3 * 2 * 256 * 2048 * 640, bytes_accessed=8 * 2**20, transcendentals=0
        ),
    )(*blocks)


def spread_kernel(w_hbm, o_ref, held, sem):
    copy = pltpu.make_async_copy(w_hbm.at[:, pl.ds(2 * lax.axis_index("core"), 2)], held, sem)
    copy.start()
    copy.wait()
    for y in range(8):
        o_ref[pl.ds(y * 8, 8)] = held[...]


def spread(w):
    return pl.pallas_call(
        spread_kernel,
        in_specs=[pl.BlockSpec(memory_space=pl.ANY)],
        out_specs=VMEM,
        out_shape=jax.ShapeDtypeStruct((64, 2, 8, 128), F32),
        scratch_shapes=[pltpu.VMEM((8, 2, 8, 128), F32), pltpu.SemaphoreType.DMA],
        compiler_params=pltpu.CompilerParams(vmem_limit_bytes=SPREAD_LIMIT),
        cost_estimate=pl.CostEstimate(flops=0, bytes_accessed=2**20, transcendentals=0),
    )(w.reshape(8, 4, 8, 128))


def pack_kernel(part_ref, c0, c1, c2, c3, o_ref, ladder_sum, cycle_sum):
    ladder_sum[...] = part_ref[0] + part_ref[1]
    cycle_sum[...] = (c0[...] + c1[...]) + (c2[...] + c3[...])
    for d in range(64):
        o_ref[d, :, pl.ds(0, 640)] = ladder_sum[pl.ds(2 * d, 2), :]
        o_ref[d, :, pl.ds(640, 256)] = cycle_sum[pl.ds(d // 4 * 2, 2), :]


def finish_kernel(p_ref, ladder_ref, cycle_ref):
    zh = lax.axis_index("zh")
    total = [p_ref[d, :, pl.ds(0, 640)] for d in range(8)]
    for d in range(8, 64):
        total[d % 8] += p_ref[d, :, pl.ds(0, 640)]
    while len(total) > 1:
        total = [p + q for p, q in zip(total[::2], total[1::2])]
    ladder_ref[...] = total[0]
    for y in range(8):
        cycle_ref[y] = (
            p_ref[y * 8 + zh, :, pl.ds(640, 256)] + p_ref[y * 8 + 4 + zh, :, pl.ds(640, 256)]
        )


def cycle_kernel(occ_ref, a_ref, own_ref, other_ref, vir_ref, pair_ref, o_ref, turned):
    first = (lax.axis_index("zl") * 4 + lax.axis_index("x")) * 4
    core = lax.axis_index("core")
    total = jnp.zeros((256, 128), F32)
    for half, w_ref in ((core, own_ref), (1 - core, other_ref)):
        for s in range(2):
            k = 2 * half + s
            allowed = jnp.bitwise_xor(vir_ref[...], occ_ref[first + k]) == pair_ref[...]
            w = jnp.where(allowed, w_ref[:, s].reshape(512, 128), 0.0)
            ah, al = split(a_ref[:, k].reshape(256, 512))
            wh, wl = split(w)
            total = total + dot3(ah, al, wh, wl)
    turned[...] = total.T
    for x in range(4):
        to = lax.rem(x + 4 - lax.axis_index("x"), 4)
        for d in range(16):
            o_ref[to, pl.ds(2 * d, 2), :] = turned[pl.ds(8 * d + 2 * x, 2), :]


def cycle(occ, amplitudes, own, other, vir, pair):
    return pl.pallas_call(
        cycle_kernel,
        in_specs=[pl.BlockSpec(memory_space=pltpu.SMEM)] + [VMEM] * 5,
        out_specs=VMEM,
        out_shape=jax.ShapeDtypeStruct((4, 32, 256), F32),
        scratch_shapes=[pltpu.VMEM((128, 256), F32)],
        compiler_params=pltpu.CompilerParams(vmem_limit_bytes=VMEM_LIMIT),
        cost_estimate=pl.CostEstimate(
            flops=3 * 2 * 256 * 2048 * 128, bytes_accessed=3 * 2**20, transcendentals=0
        ),
    )(occ, amplitudes, own, other, vir, pair)


def exchange(v, axes):
    return lax.all_to_all(v, axes, split_axis=0, concat_axis=0, tiled=True)


def body(amplitudes, ladder_ints, cycle_ints, occ_irrep, vir_irrep, pair_irrep):
    own = exchange(spread(cycle_ints), ("y", "zl", "x"))

    ring = [[(i, (i + s) % 4) for i in range(4)] for s in range(4)]
    sent = regroup(amplitudes)
    _, ladder_ints = lax.optimization_barrier((sent, ladder_ints))
    sent, own = lax.optimization_barrier((sent, own))
    x = exchange(sent, ("y", "zl"))
    other = lax.ppermute(own, "core", [(0, 1), (1, 0)])
    lower, upper = ladder_ints[:32], ladder_ints[32:]
    b1 = lax.ppermute(lower, "x", ring[1])
    b3_far = lax.ppermute(upper, "x", ring[3])
    b1_far = lax.ppermute(upper, "x", ring[1])
    b3 = lax.ppermute(lower, "x", ring[3])
    near = lax.ppermute(b1, "x", ring[1])
    far = lax.ppermute(b3_far, "x", ring[3])

    vir = jnp.broadcast_to(vir_irrep[:, None], (512, 128))
    parts = cycle(occ_irrep, amplitudes, own, other, vir, pair_irrep[None])
    parts = [parts[0]] + [lax.ppermute(parts[s], "x", ring[s]) for s in (1, 2, 3)]

    part = ladder(b1, b1_far, b3, near, x, ladder_ints, b3_far, far)
    part = exchange(part, ("core",))
    both = small(pack_kernel, (64, 2, 896), part, *parts, scratch=[(128, 640), (32, 256)])
    both = exchange(both, ("y", "zl", "zh"))
    part, cycle_part = small(finish_kernel, [(2, 640), (8, 2, 256)], both)
    cycle_resid = cycle_part.reshape(8, 2, 4, 64).transpose(0, 2, 3, 1).reshape(32, 64, 2)
    move = [
        ((s * 4 + a) * 4 + hi * 2 + lo, (hi * 4 + lo * 2 + s) * 4 + a)
        for s in range(2)
        for a in range(4)
        for hi in range(2)
        for lo in range(2)
    ]
    ladder_resid = lax.ppermute(part, ("zl", "x", "zh"), move)
    return ladder_resid, cycle_resid


def solution(mesh):
    fine = Mesh(mesh.devices.reshape(8, 2, 4, 4, 2), ("y", "zl", "x", "zh", "core"))
    col, depth = ("zl", "x"), ("zh", "core")
    in_specs = (
        P("y", col, depth, None),
        P(depth, ("y", "zl", "x"), None),
        P(None, ("y", "zl", "x"), None),
        P(),
        P(),
        P(),
    )
    out_specs = (P(("y", "zl", "x", "zh", "core"), None), P(None, depth, ("y", "zl", "x")))
    return jax.shard_map(body, mesh=fine, in_specs=in_specs, out_specs=out_specs, check_vma=False)
```

```python
import jax
import jax.numpy as jnp
from jax import lax
from jax.experimental import pallas as pl
from jax.experimental.pallas import tpu as pltpu
from jax.sharding import Mesh, PartitionSpec as P

F32 = jnp.float32
BF16 = jnp.bfloat16
VMEM_LIMIT = 16 * 1024 * 1024
LADDER_LIMIT = 51 * 1024 * 1024
SPREAD_LIMIT = 60 * 1024 * 1024


def split(v):
    hi = v.astype(BF16)
    lo = (v - hi.astype(F32)).astype(BF16)
    return hi, lo


def dot3(xh, xl, bh, bl):
    def mm(p, q):
        return jnp.dot(p, q, preferred_element_type=F32)

    return mm(xh, bh) + (mm(xh, bl) + mm(xl, bh))


def regroup_kernel(a_ref, o_ref):
    rows = a_ref.reshape(512, 128)
    lane = lax.broadcasted_iota(jnp.int32, (8, 128), 1)
    low = lane < 64
    even = (lane & 32) == 0

    def swap(keep, p, q, width):
        return (
            jnp.where(keep, p, pltpu.roll(q, width, 1)),
            jnp.where(keep, pltpu.roll(p, 128 - width, 1), q),
        )

    for q in range(16):
        v = [rows[pl.ds(4 * q + c, 8, stride=64), :] for c in range(4)]
        t0, t2 = swap(low, v[0], v[2], 64)
        t1, t3 = swap(low, v[1], v[3], 64)
        o0, o1 = swap(even, t0, t1, 32)
        o2, o3 = swap(even, t2, t3, 32)
        for g, o in enumerate((o0, o1, o2, o3)):
            o_ref[g, :, pl.ds(q * 128, 128)] = o


def regroup(amplitudes):
    a = amplitudes.reshape(4, 2, 2, 64, 512)
    return pl.pallas_call(
        regroup_kernel,
        grid=(4, 2),
        in_specs=[pl.BlockSpec((4, None, 2, 64, 128), lambda b, h: (0, h, 0, 0, b))],
        out_specs=pl.BlockSpec((4, None, 8, 2048), lambda b, h: (b, h, 0, 0)),
        out_shape=jax.ShapeDtypeStruct((16, 2, 8, 2048), F32),
        compiler_params=pltpu.CompilerParams(vmem_limit_bytes=VMEM_LIMIT),
        cost_estimate=pl.CostEstimate(flops=2**20, bytes_accessed=2**22, transcendentals=0),
    )(a)


def ladder_kernel(b1, b1_far, b3, near, x_hbm, b0, b3_far, far, o_ref, x_ref, held, sems):
    me = lax.axis_index("x")
    pieces = ((0, 8), (8, 8), (16, 16), (32, 16), (48, 16))

    def copies(k, c, size):
        part, half, span = pl.ds(c, size), pl.ds(c % 32, size), pl.ds(c * 32, size * 32)
        found = [(0, b0.at[part])]
        if c >= 32:
            found += [(1, b3_far.at[half]), (2, far.at[half])]
        return [
            pltpu.make_async_copy(x_hbm.at[:, :, :, span], x_ref.at[:, :, :, span], sems.at[3, k])
        ] + [
            pltpu.make_async_copy(b, held.at[lax.rem(me + s, 4), part], sems.at[s, k])
            for s, b in found
        ]

    for k, (c, size) in enumerate(pieces):
        for copy in copies(k, c, size):
            copy.start()
    for k, (c, size) in enumerate(pieces):
        part, half, span = pl.ds(c, size), pl.ds(c % 32, size), pl.ds(c * 32, size * 32)
        held[lax.rem(me + 3, 4), part] = (b1 if c < 32 else b1_far)[half]
        if c < 32:
            held[lax.rem(me + 1, 4), part] = b3[half]
            held[lax.rem(me + 2, 4), part] = near[half]
        for copy in copies(k, c, size):
            copy.wait()
        rows = [x_ref[:, h, :, span].reshape(128, size * 32) for h in range(2)]
        xh, xl = split(jnp.concatenate(rows, axis=0))
        b = [held[o, c + d] for d in range(size) for o in range(4)]
        bh, bl = split(jnp.concatenate(b, axis=0))
        total = dot3(xh, xl, bh, bl).reshape(2, 128, 640)
        if k == 0:
            o_ref[...] = total
        else:
            o_ref[...] += total


VMEM = pl.BlockSpec(memory_space=pltpu.VMEM)


def small(kernel, out_shape, *args, scratch=()):
    return pl.pallas_call(
        kernel,
        in_specs=[VMEM] * len(args),
        out_specs=VMEM if isinstance(out_shape, tuple) else [VMEM] * len(out_shape),
        out_shape=jax.ShapeDtypeStruct(out_shape, F32)
        if isinstance(out_shape, tuple)
        else [jax.ShapeDtypeStruct(shape, F32) for shape in out_shape],
        scratch_shapes=[pltpu.VMEM(shape, F32) for shape in scratch],
        compiler_params=pltpu.CompilerParams(vmem_limit_bytes=VMEM_LIMIT),
        cost_estimate=pl.CostEstimate(flops=2**18, bytes_accessed=2**20, transcendentals=0),
    )(*args)


def ladder(*blocks):
    anywhere = pl.BlockSpec(memory_space=pl.ANY)
    return pl.pallas_call(
        ladder_kernel,
        in_specs=[VMEM] * 4 + [anywhere] * 4,
        out_specs=VMEM,
        out_shape=jax.ShapeDtypeStruct((2, 128, 640), F32),
        scratch_shapes=[
            pltpu.VMEM((16, 2, 8, 2048), F32),
            pltpu.VMEM((4, 64, 8, 640), F32),
            pltpu.SemaphoreType.DMA((4, 5)),
        ],
        compiler_params=pltpu.CompilerParams(vmem_limit_bytes=LADDER_LIMIT),
        cost_estimate=pl.CostEstimate(
            flops=3 * 2 * 256 * 2048 * 640, bytes_accessed=8 * 2**20, transcendentals=0
        ),
    )(*blocks)


def spread_kernel(w_hbm, o_ref, held, sem):
    copy = pltpu.make_async_copy(w_hbm.at[:, pl.ds(2 * lax.axis_index("core"), 2)], held, sem)
    copy.start()
    copy.wait()
    for y in range(8):
        o_ref[pl.ds(y * 8, 8)] = held[...]


def spread(w):
    return pl.pallas_call(
        spread_kernel,
        in_specs=[pl.BlockSpec(memory_space=pl.ANY)],
        out_specs=VMEM,
        out_shape=jax.ShapeDtypeStruct((64, 2, 8, 128), F32),
        scratch_shapes=[pltpu.VMEM((8, 2, 8, 128), F32), pltpu.SemaphoreType.DMA],
        compiler_params=pltpu.CompilerParams(vmem_limit_bytes=SPREAD_LIMIT),
        cost_estimate=pl.CostEstimate(flops=0, bytes_accessed=2**20, transcendentals=0),
    )(w.reshape(8, 4, 8, 128))


def pack_kernel(part_ref, c0, c1, c2, c3, o_ref, ladder_sum, cycle_sum):
    ladder_sum[...] = part_ref[0] + part_ref[1]
    cycle_sum[...] = (c0[...] + c1[...]) + (c2[...] + c3[...])
    for d in range(64):
        o_ref[d, :, pl.ds(0, 640)] = ladder_sum[pl.ds(2 * d, 2), :]
        o_ref[d, :, pl.ds(640, 256)] = cycle_sum[pl.ds(d // 4 * 2, 2), :]


def finish_kernel(p_ref, ladder_ref, cycle_ref):
    zh = lax.axis_index("zh")
    total = [p_ref[d, :, pl.ds(0, 640)] for d in range(8)]
    for d in range(8, 64):
        total[d % 8] += p_ref[d, :, pl.ds(0, 640)]
    while len(total) > 1:
        total = [p + q for p, q in zip(total[::2], total[1::2])]
    ladder_ref[...] = total[0]
    for y in range(8):
        cycle_ref[y] = (
            p_ref[y * 8 + zh, :, pl.ds(640, 256)] + p_ref[y * 8 + 4 + zh, :, pl.ds(640, 256)]
        )


def cycle_kernel(occ_ref, a_ref, own_ref, other_ref, vir_ref, pair_ref, o_ref, turned):
    first = (lax.axis_index("zl") * 4 + lax.axis_index("x")) * 4
    core = lax.axis_index("core")
    total = jnp.zeros((256, 128), F32)
    for half, w_ref in ((core, own_ref), (1 - core, other_ref)):
        for s in range(2):
            k = 2 * half + s
            allowed = jnp.bitwise_xor(vir_ref[...], occ_ref[first + k]) == pair_ref[...]
            w = jnp.where(allowed, w_ref[:, s].reshape(512, 128), 0.0)
            ah, al = split(a_ref[:, k].reshape(256, 512))
            wh, wl = split(w)
            total = total + dot3(ah, al, wh, wl)
    turned[...] = total.T
    for x in range(4):
        to = lax.rem(x + 4 - lax.axis_index("x"), 4)
        for d in range(16):
            o_ref[to, pl.ds(2 * d, 2), :] = turned[pl.ds(8 * d + 2 * x, 2), :]


def cycle(occ, amplitudes, own, other, vir, pair):
    return pl.pallas_call(
        cycle_kernel,
        in_specs=[pl.BlockSpec(memory_space=pltpu.SMEM)] + [VMEM] * 5,
        out_specs=VMEM,
        out_shape=jax.ShapeDtypeStruct((4, 32, 256), F32),
        scratch_shapes=[pltpu.VMEM((128, 256), F32)],
        compiler_params=pltpu.CompilerParams(vmem_limit_bytes=VMEM_LIMIT),
        cost_estimate=pl.CostEstimate(
            flops=3 * 2 * 256 * 2048 * 128, bytes_accessed=3 * 2**20, transcendentals=0
        ),
    )(occ, amplitudes, own, other, vir, pair)


def exchange(v, axes):
    return lax.all_to_all(v, axes, split_axis=0, concat_axis=0, tiled=True)


def body(amplitudes, ladder_ints, cycle_ints, occ_irrep, vir_irrep, pair_irrep):
    own = exchange(spread(cycle_ints), ("y", "zl", "x"))

    ring = [[(i, (i + s) % 4) for i in range(4)] for s in range(4)]
    sent = regroup(amplitudes)
    _, ladder_ints = lax.optimization_barrier((sent, ladder_ints))
    sent, own = lax.optimization_barrier((sent, own))
    x = exchange(sent, ("y", "zl"))
    other = lax.ppermute(own, "core", [(0, 1), (1, 0)])
    lower, upper = ladder_ints[:32], ladder_ints[32:]
    b1 = lax.ppermute(lower, "x", ring[1])
    b3_far = lax.ppermute(upper, "x", ring[3])
    b1_far = lax.ppermute(upper, "x", ring[1])
    b3 = lax.ppermute(lower, "x", ring[3])
    near = lax.ppermute(b1, "x", ring[1])
    far = lax.ppermute(b3_far, "x", ring[3])

    vir = jnp.broadcast_to(vir_irrep[:, None], (512, 128))
    parts = cycle(occ_irrep, amplitudes, own, other, vir, pair_irrep[None])
    parts = [parts[0]] + [lax.ppermute(parts[s], "x", ring[s]) for s in (1, 2, 3)]

    part = ladder(b1, b1_far, b3, near, x, ladder_ints, b3_far, far)
    part = exchange(part, ("core",))
    both = small(pack_kernel, (64, 2, 896), part, *parts, scratch=[(128, 640), (32, 256)])
    both = exchange(both, ("y", "zl", "zh"))
    part, cycle_part = small(finish_kernel, [(2, 640), (8, 2, 256)], both)
    cycle_resid = cycle_part.reshape(8, 2, 4, 64).transpose(0, 2, 3, 1).reshape(32, 64, 2)
    move = [
        ((s * 4 + a) * 4 + hi * 2 + lo, (hi * 4 + lo * 2 + s) * 4 + a)
        for s in range(2)
        for a in range(4)
        for hi in range(2)
        for lo in range(2)
    ]
    ladder_resid = lax.ppermute(part, ("zl", "x", "zh"), move)
    return ladder_resid, cycle_resid


def solution(mesh):
    fine = Mesh(mesh.devices.reshape(8, 2, 4, 4, 2), ("y", "zl", "x", "zh", "core"))
    col, depth = ("zl", "x"), ("zh", "core")
    in_specs = (
        P("y", col, depth, None),
        P(depth, ("y", "zl", "x"), None),
        P(None, ("y", "zl", "x"), None),
        P(),
        P(),
        P(),
    )
    out_specs = (P(("y", "zl", "x", "zh", "core"), None), P(None, depth, ("y", "zl", "x")))
    return jax.shard_map(body, mesh=fine, in_specs=in_specs, out_specs=out_specs, check_vma=False)
```

```python
import jax
import jax.numpy as jnp
from jax import lax
from jax.experimental import pallas as pl
from jax.experimental.pallas import tpu as pltpu
from jax.sharding import Mesh, PartitionSpec as P

F32 = jnp.float32
BF16 = jnp.bfloat16
VMEM_LIMIT = 16 * 1024 * 1024
LADDER_LIMIT = 51 * 1024 * 1024
SPREAD_LIMIT = 60 * 1024 * 1024


def split(v):
    hi = v.astype(BF16)
    lo = (v - hi.astype(F32)).astype(BF16)
    return hi, lo


def dot3(xh, xl, bh, bl):
    def mm(p, q):
        return jnp.dot(p, q, preferred_element_type=F32)

    return mm(xh, bh) + (mm(xh, bl) + mm(xl, bh))


def regroup_kernel(a_ref, o_ref):
    rows = a_ref.reshape(512, 128)
    lane = lax.broadcasted_iota(jnp.int32, (8, 128), 1)
    low = lane < 64
    even = (lane & 32) == 0

    def swap(keep, p, q, width):
        return (
            jnp.where(keep, p, pltpu.roll(q, width, 1)),
            jnp.where(keep, pltpu.roll(p, 128 - width, 1), q),
        )

    for q in range(16):
        v = [rows[pl.ds(4 * q + c, 8, stride=64), :] for c in range(4)]
        t0, t2 = swap(low, v[0], v[2], 64)
        t1, t3 = swap(low, v[1], v[3], 64)
        o0, o1 = swap(even, t0, t1, 32)
        o2, o3 = swap(even, t2, t3, 32)
        for g, o in enumerate((o0, o1, o2, o3)):
            o_ref[g, :, pl.ds(q * 128, 128)] = o


def regroup(amplitudes):
    a = amplitudes.reshape(4, 2, 2, 64, 512)
    return pl.pallas_call(
        regroup_kernel,
        grid=(4, 2),
        in_specs=[pl.BlockSpec((4, None, 2, 64, 128), lambda b, h: (0, h, 0, 0, b))],
        out_specs=pl.BlockSpec((4, None, 8, 2048), lambda b, h: (b, h, 0, 0)),
        out_shape=jax.ShapeDtypeStruct((16, 2, 8, 2048), F32),
        compiler_params=pltpu.CompilerParams(vmem_limit_bytes=VMEM_LIMIT),
        cost_estimate=pl.CostEstimate(flops=2**20, bytes_accessed=2**22, transcendentals=0),
    )(a)


def ladder_kernel(b1, b1_far, b3, near, x_hbm, b0, b3_far, far, o_ref, x_ref, held, sems):
    me = lax.axis_index("x")
    pieces = ((0, 8), (8, 12), (20, 16), (36, 16), (52, 12))

    def copies(k, c, size):
        part, half, span = pl.ds(c, size), pl.ds(c % 36, size), pl.ds(c * 32, size * 32)
        found = [(0, b0.at[part])]
        if c >= 36:
            found += [(1, b3_far.at[half]), (2, far.at[half])]
        return [
            pltpu.make_async_copy(x_hbm.at[:, :, :, span], x_ref.at[:, :, :, span], sems.at[3, k])
        ] + [
            pltpu.make_async_copy(b, held.at[lax.rem(me + s, 4), part], sems.at[s, k])
            for s, b in found
        ]

    for k, (c, size) in enumerate(pieces):
        for copy in copies(k, c, size):
            copy.start()
    for k, (c, size) in enumerate(pieces):
        part, half, span = pl.ds(c, size), pl.ds(c % 36, size), pl.ds(c * 32, size * 32)
        held[lax.rem(me + 3, 4), part] = (b1 if c < 36 else b1_far)[half]
        if c < 36:
            held[lax.rem(me + 1, 4), part] = b3[half]
            held[lax.rem(me + 2, 4), part] = near[half]
        for copy in copies(k, c, size):
            copy.wait()
        rows = [x_ref[:, h, :, span].reshape(128, size * 32) for h in range(2)]
        xh, xl = split(jnp.concatenate(rows, axis=0))
        b = [held[o, c + d] for d in range(size) for o in range(4)]
        bh, bl = split(jnp.concatenate(b, axis=0))
        total = dot3(xh, xl, bh, bl).reshape(2, 128, 640)
        if k == 0:
            o_ref[...] = total
        else:
            o_ref[...] += total


VMEM = pl.BlockSpec(memory_space=pltpu.VMEM)


def small(kernel, out_shape, *args, scratch=()):
    return pl.pallas_call(
        kernel,
        in_specs=[VMEM] * len(args),
        out_specs=VMEM if isinstance(out_shape, tuple) else [VMEM] * len(out_shape),
        out_shape=jax.ShapeDtypeStruct(out_shape, F32)
        if isinstance(out_shape, tuple)
        else [jax.ShapeDtypeStruct(shape, F32) for shape in out_shape],
        scratch_shapes=[pltpu.VMEM(shape, F32) for shape in scratch],
        compiler_params=pltpu.CompilerParams(vmem_limit_bytes=VMEM_LIMIT),
        cost_estimate=pl.CostEstimate(flops=2**18, bytes_accessed=2**20, transcendentals=0),
    )(*args)


def ladder(*blocks):
    anywhere = pl.BlockSpec(memory_space=pl.ANY)
    return pl.pallas_call(
        ladder_kernel,
        in_specs=[VMEM] * 4 + [anywhere] * 4,
        out_specs=VMEM,
        out_shape=jax.ShapeDtypeStruct((2, 128, 640), F32),
        scratch_shapes=[
            pltpu.VMEM((16, 2, 8, 2048), F32),
            pltpu.VMEM((4, 64, 8, 640), F32),
            pltpu.SemaphoreType.DMA((4, 5)),
        ],
        compiler_params=pltpu.CompilerParams(vmem_limit_bytes=LADDER_LIMIT),
        cost_estimate=pl.CostEstimate(
            flops=3 * 2 * 256 * 2048 * 640, bytes_accessed=8 * 2**20, transcendentals=0
        ),
    )(*blocks)


def spread_kernel(w_hbm, o_ref, held, sem):
    copy = pltpu.make_async_copy(w_hbm.at[:, pl.ds(2 * lax.axis_index("core"), 2)], held, sem)
    copy.start()
    copy.wait()
    for y in range(8):
        o_ref[pl.ds(y * 8, 8)] = held[...]


def spread(w):
    return pl.pallas_call(
        spread_kernel,
        in_specs=[pl.BlockSpec(memory_space=pl.ANY)],
        out_specs=VMEM,
        out_shape=jax.ShapeDtypeStruct((64, 2, 8, 128), F32),
        scratch_shapes=[pltpu.VMEM((8, 2, 8, 128), F32), pltpu.SemaphoreType.DMA],
        compiler_params=pltpu.CompilerParams(vmem_limit_bytes=SPREAD_LIMIT),
        cost_estimate=pl.CostEstimate(flops=0, bytes_accessed=2**20, transcendentals=0),
    )(w.reshape(8, 4, 8, 128))


def pack_kernel(part_ref, c0, c1, c2, c3, o_ref, ladder_sum, cycle_sum):
    ladder_sum[...] = part_ref[0] + part_ref[1]
    cycle_sum[...] = (c0[...] + c1[...]) + (c2[...] + c3[...])
    for d in range(64):
        o_ref[d, :, pl.ds(0, 640)] = ladder_sum[pl.ds(2 * d, 2), :]
        o_ref[d, :, pl.ds(640, 256)] = cycle_sum[pl.ds(d // 4 * 2, 2), :]


def finish_kernel(p_ref, ladder_ref, cycle_ref):
    zh = lax.axis_index("zh")
    total = [p_ref[d, :, pl.ds(0, 640)] for d in range(8)]
    for d in range(8, 64):
        total[d % 8] += p_ref[d, :, pl.ds(0, 640)]
    while len(total) > 1:
        total = [p + q for p, q in zip(total[::2], total[1::2])]
    ladder_ref[...] = total[0]
    for y in range(8):
        cycle_ref[y] = (
            p_ref[y * 8 + zh, :, pl.ds(640, 256)] + p_ref[y * 8 + 4 + zh, :, pl.ds(640, 256)]
        )


def cycle_kernel(occ_ref, a_ref, own_ref, other_ref, vir_ref, pair_ref, o_ref, turned):
    first = (lax.axis_index("zl") * 4 + lax.axis_index("x")) * 4
    core = lax.axis_index("core")
    total = jnp.zeros((256, 128), F32)
    for half, w_ref in ((core, own_ref), (1 - core, other_ref)):
        for s in range(2):
            k = 2 * half + s
            allowed = jnp.bitwise_xor(vir_ref[...], occ_ref[first + k]) == pair_ref[...]
            w = jnp.where(allowed, w_ref[:, s].reshape(512, 128), 0.0)
            ah, al = split(a_ref[:, k].reshape(256, 512))
            wh, wl = split(w)
            total = total + dot3(ah, al, wh, wl)
    turned[...] = total.T
    for x in range(4):
        to = lax.rem(x + 4 - lax.axis_index("x"), 4)
        for d in range(16):
            o_ref[to, pl.ds(2 * d, 2), :] = turned[pl.ds(8 * d + 2 * x, 2), :]


def cycle(occ, amplitudes, own, other, vir, pair):
    return pl.pallas_call(
        cycle_kernel,
        in_specs=[pl.BlockSpec(memory_space=pltpu.SMEM)] + [VMEM] * 5,
        out_specs=VMEM,
        out_shape=jax.ShapeDtypeStruct((4, 32, 256), F32),
        scratch_shapes=[pltpu.VMEM((128, 256), F32)],
        compiler_params=pltpu.CompilerParams(vmem_limit_bytes=VMEM_LIMIT),
        cost_estimate=pl.CostEstimate(
            flops=3 * 2 * 256 * 2048 * 128, bytes_accessed=3 * 2**20, transcendentals=0
        ),
    )(occ, amplitudes, own, other, vir, pair)


def exchange(v, axes):
    return lax.all_to_all(v, axes, split_axis=0, concat_axis=0, tiled=True)


def body(amplitudes, ladder_ints, cycle_ints, occ_irrep, vir_irrep, pair_irrep):
    own = exchange(spread(cycle_ints), ("y", "zl", "x"))

    ring = [[(i, (i + s) % 4) for i in range(4)] for s in range(4)]
    sent = regroup(amplitudes)
    _, ladder_ints = lax.optimization_barrier((sent, ladder_ints))
    sent, own = lax.optimization_barrier((sent, own))
    x = exchange(sent, ("y", "zl"))
    other = lax.ppermute(own, "core", [(0, 1), (1, 0)])
    lower, upper = ladder_ints[:36], ladder_ints[36:]
    b1 = lax.ppermute(lower, "x", ring[1])
    b3_far = lax.ppermute(upper, "x", ring[3])
    b1_far = lax.ppermute(upper, "x", ring[1])
    b3 = lax.ppermute(lower, "x", ring[3])
    near = lax.ppermute(b1, "x", ring[1])
    far = lax.ppermute(b3_far, "x", ring[3])

    vir = jnp.broadcast_to(vir_irrep[:, None], (512, 128))
    parts = cycle(occ_irrep, amplitudes, own, other, vir, pair_irrep[None])
    parts = [parts[0]] + [lax.ppermute(parts[s], "x", ring[s]) for s in (1, 2, 3)]

    part = ladder(b1, b1_far, b3, near, x, ladder_ints, b3_far, far)
    part = exchange(part, ("core",))
    both = small(pack_kernel, (64, 2, 896), part, *parts, scratch=[(128, 640), (32, 256)])
    both = exchange(both, ("y", "zl", "zh"))
    part, cycle_part = small(finish_kernel, [(2, 640), (8, 2, 256)], both)
    cycle_resid = cycle_part.reshape(8, 2, 4, 64).transpose(0, 2, 3, 1).reshape(32, 64, 2)
    move = [
        ((s * 4 + a) * 4 + hi * 2 + lo, (hi * 4 + lo * 2 + s) * 4 + a)
        for s in range(2)
        for a in range(4)
        for hi in range(2)
        for lo in range(2)
    ]
    ladder_resid = lax.ppermute(part, ("zl", "x", "zh"), move)
    return ladder_resid, cycle_resid


def solution(mesh):
    fine = Mesh(mesh.devices.reshape(8, 2, 4, 4, 2), ("y", "zl", "x", "zh", "core"))
    col, depth = ("zl", "x"), ("zh", "core")
    in_specs = (
        P("y", col, depth, None),
        P(depth, ("y", "zl", "x"), None),
        P(None, ("y", "zl", "x"), None),
        P(),
        P(),
        P(),
    )
    out_specs = (P(("y", "zl", "x", "zh", "core"), None), P(None, depth, ("y", "zl", "x")))
    return jax.shard_map(body, mesh=fine, in_specs=in_specs, out_specs=out_specs, check_vma=False)
```
